256 devices in a mesh: dp: 4 (over x_hi, core), ctx: 16 (over z, x_lo), tensor: 4 (over y).
Axes of the slice: x: 4 (x_hi: 2, x_lo: 2; x = x_hi * 2 + x_lo), y: 4, z: 8, core: 2. Of those that a mesh axis runs over, the one named last changes fastest.
Arguments:
- query_latent: bfloat16 [4, 8192, 1536], P('dp', 'ctx'), may hold values from -6 to 6
- shared_latent: bfloat16 [4, 8192, 512], P('dp', 'ctx'), may hold values from -6 to 6
- rope_keys: bfloat16 [4, 8192, 64], P('dp', 'ctx'), may hold values from -6 to 6
- block_order: int32 [4, 16], replicated, may hold values from 0 to 15, each once within a row
- query_weight: bfloat16 [1536, 12288], P(('dp', 'ctx'), 'tensor'), as said below
- key_weight: bfloat16 [512, 8192], P(('dp', 'ctx'), 'tensor'), may hold values from -0.25 to 0.25
- value_weight: bfloat16 [512, 8192], P(('dp', 'ctx'), 'tensor'), may hold values from -0.25 to 0.25
Outputs:
- attended: bfloat16 [4, 8192, 8192], P('dp', 'ctx', 'tensor')
- logit_max: float32 [64], P('tensor')
- clipped_query_weight: bfloat16 [1536, 12288], P(('dp', 'ctx'), 'tensor')
- clipped_key_weight: bfloat16 [512, 8192], P(('dp', 'ctx'), 'tensor')
The draws below stay inside these ranges and needn't reach their ends.
Inputs may be any that keep to these rules, and one draw needn't show every extreme that they name: `block_order`: each row is a permutation: every block of a sequence is held by exactly one ctx index. `query_weight`: entries of each head's columns have a head-dependent spread.
All inputs are finite; a program needn't handle non-finite values.
Results may differ from the reference program's by a relative error of at most 0.012.
The reference program's roundings to bfloat16 on the way count: a program that leaves them out, or rounds other values in their place, can miss the bound.
Values may be sent and summed in bfloat16 or wider, within the bound.
No kernel may reach another device: no remote copies, remote signals or barrier semaphores. Data moves between devices by JAX's collectives and lax.ppermute only.
A program may use at most 128 MiB of HBM per device.

```python
import math
import jax
import jax.numpy as jnp
from jax import lax

H = 64
QK_NOPE = 128
QK_ROPE = 64
V_DIM = 128
KL = 512
QL = 1536
TOK_DEV = 512
TAU = 100
TOKENS = 8192
SEQS = 4
N_CTX = 16


def draw_query_weight(key, part):
    key = jax.random.fold_in(key, 7)
    scale_key, entry_key = jax.random.split(key)
    head_scales = jnp.exp(jax.random.uniform(scale_key, (H,), jnp.float32, math.log(2.0), math.log(40.0)))
    entries = jax.random.truncated_normal(entry_key, -4.0, 4.0, (QL, H, QK_NOPE + QK_ROPE), jnp.float32)
    return (entries * head_scales[None, :, None] / math.sqrt(QL)).reshape(QL, H * (QK_NOPE + QK_ROPE)).astype(jnp.bfloat16)


def steps_of(key, shape, pieces, low, largest):
    loudness, own = 1.0, jax.random.fold_in(key, 6)
    for dim, blocks in pieces:
        steps = jnp.exp(jax.random.uniform(jax.random.fold_in(own, dim), (blocks,), jnp.float32, low / len(pieces), largest / len(pieces)))
        loudness = loudness * jnp.repeat(steps, shape[dim] // blocks).reshape([-1 if axis == dim else 1 for axis in range(len(shape))])
    return loudness


def normal_values(stream_key, extent, width, bound, cuts=(), kind=jnp.bfloat16):
    drawn = jax.random.normal(stream_key, extent, jnp.float32) * width
    if len(cuts) > 0:
        drawn = steps_of(stream_key, extent, cuts, -0.22, 0.18) * drawn
    return jnp.clip(drawn, min=-bound, max=bound).astype(kind)


def setup_inputs(seed: int = 0) -> dict:
    arg_keys = jax.random.split(jax.random.key(seed), 8)
    query_latent = normal_values(arg_keys[0], (SEQS, TOKENS, QL), 1.0, 6.0, ((0, 4), (1, 16)))
    shared_latent = normal_values(arg_keys[1], (SEQS, TOKENS, KL), 1.0, 6.0, ((0, 4), (1, 16)))
    rope_keys = normal_values(arg_keys[2], (SEQS, TOKENS, QK_ROPE), 1.0, 6.0, ((0, 4), (1, 16)))
    block_order = jax.vmap(lambda own: jax.random.permutation(own, N_CTX))(jax.random.split(arg_keys[3], SEQS)).reshape((SEQS, N_CTX)).astype(jnp.int32)
    query_weight = draw_query_weight(jax.random.fold_in(arg_keys[7], 71), 0)
    key_weight = normal_values(arg_keys[5], (KL, H * QK_NOPE), KL ** -0.5, 0.25, ((0, 64), (1, 4)))
    value_weight = normal_values(arg_keys[6], (KL, H * V_DIM), KL ** -0.5, 0.25, ((0, 64), (1, 4)))
    return dict(query_latent=query_latent, shared_latent=shared_latent, rope_keys=rope_keys, block_order=block_order, query_weight=query_weight, key_weight=key_weight, value_weight=value_weight)


def head_attend(query_head, key_head, rope_block, value_head, allowed):
    logit_scale = 1.0 / math.sqrt(QK_NOPE + QK_ROPE)
    plain = jnp.dot(query_head[:, :QK_NOPE], key_head.T, preferred_element_type=jnp.float32)
    rotated = jnp.dot(query_head[:, QK_NOPE:], rope_block.T, preferred_element_type=jnp.float32)
    logits = (plain + rotated) * logit_scale
    masked = jnp.where(allowed, logits, -jnp.inf)
    head_peak = jnp.max(masked)
    row_peak = lax.optimization_barrier(jnp.max(masked, axis=1, keepdims=True))
    expos = jnp.exp(masked - row_peak)
    probabilities = (expos / lax.optimization_barrier(jnp.sum(expos, axis=1, keepdims=True))).astype(jnp.bfloat16)
    result = jnp.dot(probabilities, value_head, preferred_element_type=jnp.float32).astype(jnp.bfloat16)
    return (result, head_peak)

def reference(query_latent, shared_latent, rope_keys, block_order, query_weight, key_weight, value_weight):
    head_width = QK_NOPE + QK_ROPE
    offsets = jnp.arange(TOK_DEV, dtype=jnp.int32)

    def one_block(block_pair):
        sequence = block_pair // N_CTX
        device = block_pair % N_CTX
        previous = (device - 1 + N_CTX) % N_CTX
        start = (device * TOK_DEV).astype(jnp.int32)
        start_prev = (previous * TOK_DEV).astype(jnp.int32)
        rows = lax.dynamic_slice_in_dim(query_latent[sequence], start, TOK_DEV, 0)
        query = jnp.dot(rows, query_weight, preferred_element_type=jnp.float32).astype(jnp.bfloat16)
        latents = jnp.concatenate([lax.dynamic_slice_in_dim(shared_latent[sequence], start, TOK_DEV, 0), lax.dynamic_slice_in_dim(shared_latent[sequence], start_prev, TOK_DEV, 0)], axis=0)
        rope_block = jnp.concatenate([lax.dynamic_slice_in_dim(rope_keys[sequence], start, TOK_DEV, 0), lax.dynamic_slice_in_dim(rope_keys[sequence], start_prev, TOK_DEV, 0)], axis=0)
        keys = jnp.dot(latents, key_weight, preferred_element_type=jnp.float32).astype(jnp.bfloat16)
        values = jnp.dot(latents, value_weight, preferred_element_type=jnp.float32).astype(jnp.bfloat16)
        order_row = block_order[sequence]
        query_place = order_row[device] * TOK_DEV + offsets
        key_place = jnp.concatenate([query_place, order_row[previous] * TOK_DEV + offsets])
        allowed = key_place[None, :] <= query_place[:, None]

        def per_head(head):
            query_head = lax.dynamic_slice_in_dim(query, head * head_width, head_width, 1)
            key_head = lax.dynamic_slice_in_dim(keys, head * QK_NOPE, QK_NOPE, 1)
            value_head = lax.dynamic_slice_in_dim(values, head * V_DIM, V_DIM, 1)
            return head_attend(query_head, key_head, rope_block, value_head, allowed)
        results, head_peaks = lax.map(per_head, jnp.arange(H, dtype=jnp.int32))
        return (jnp.transpose(results, (1, 0, 2)).reshape(TOK_DEV, H * V_DIM), head_peaks)
    blocks, peaks = lax.map(one_block, jnp.arange(SEQS * N_CTX, dtype=jnp.int32))
    attended = blocks.reshape(SEQS, N_CTX * TOK_DEV, H * V_DIM)
    logit_max = lax.optimization_barrier(jnp.max(peaks, axis=0))
    clip_factor = TAU / jnp.maximum(logit_max, TAU)
    root_factor = jnp.sqrt(clip_factor)
    column_factor = jnp.concatenate([jnp.broadcast_to(root_factor[:, None], (H, QK_NOPE)), jnp.broadcast_to(clip_factor[:, None], (H, QK_ROPE))], axis=1)
    clipped_query_weight = (query_weight.astype(jnp.float32).reshape(QL, H, head_width) * column_factor[None]).reshape(QL, H * head_width).astype(jnp.bfloat16)
    clipped_key_weight = (key_weight.astype(jnp.float32).reshape(KL, H, QK_NOPE) * root_factor[None, :, None]).reshape(KL, H * QK_NOPE).astype(jnp.bfloat16)
    return (attended, logit_max, clipped_query_weight, clipped_key_weight)
```

```python
import functools
import math

import jax
import jax.numpy as jnp
from jax import lax
from jax.experimental import pallas as pl
from jax.experimental.pallas import tpu as pltpu
from jax.sharding import Mesh
from jax.sharding import PartitionSpec as P

QK_NOPE = 128
QK_ROPE = 64
V_DIM = 128
TAU = 100
HEAD = QK_NOPE + QK_ROPE
SCALE = 1.0 / math.sqrt(HEAD)
SCALE2 = SCALE * math.log2(math.e)
FAR = 1e30

GROUP = ("xh", "core", "z", "xl")
GATHER = ("z", "xh", "xl", "core")
TOK = 512
PAIR = 2


def dot_f32(a, b):
    return jnp.dot(a, b, preferred_element_type=jnp.float32)


def dot_t(a, b):
    return lax.dot_general(a, b, (((1,), (1,)), ((), ())), preferred_element_type=jnp.float32)


def attend_kernel(seen_ref, x_ref, lat_ref, rope_ref, q0_ref, q1_ref, q2_ref, k_ref, v_ref, out_ref, peak_ref):
    half = TOK // 2
    query = dot_f32(x_ref[0], q0_ref[...]) + dot_f32(x_ref[1], q1_ref[...]) + dot_f32(x_ref[2], q2_ref[...])
    query = query.astype(jnp.bfloat16)
    keys = dot_f32(lat_ref[...], k_ref[...]).astype(jnp.bfloat16)
    values = dot_f32(lat_ref[...], v_ref[...]).astype(jnp.bfloat16)
    rope = rope_ref[...]
    seen = seen_ref[0] > 0
    row = lax.broadcasted_iota(jnp.int32, (half, half), 0)
    col = lax.broadcasted_iota(jnp.int32, (half, half), 1)
    diagonal = col <= row
    for head in range(PAIR):
        q_head = query[:, head * HEAD : (head + 1) * HEAD]
        key_head = jnp.concatenate([keys[:, head * QK_NOPE : (head + 1) * QK_NOPE], rope], axis=1)
        value_head = values[:, head * V_DIM : (head + 1) * V_DIM]
        head_peak = None
        for part in range(2):
            q_part = q_head[part * half : (part + 1) * half]
            spans = []
            if part == 1:
                spans.append((0, half, "all"))
            spans.append((part * half, half, "diag"))
            spans.append((TOK, TOK, "prev"))
            logits = []
            for start, size, kind in spans:
                s = dot_t(q_part, key_head[start : start + size])
                if kind == "diag":
                    s = jnp.where(diagonal, s, -jnp.inf)
                logits.append(s)
            peak = functools.reduce(jnp.maximum, [jnp.max(s, axis=1, keepdims=True) for s in logits[:-1]])
            prev_peak = jnp.max(logits[-1], axis=1, keepdims=True)
            peak = jnp.where(seen, jnp.maximum(peak, prev_peak), peak)
            here = jnp.max(peak)
            head_peak = here if head_peak is None else jnp.maximum(head_peak, here)
            shift = peak * SCALE2
            shift_prev = jnp.where(seen, shift, FAR)
            expos = [
                jnp.exp2(s * SCALE2 - (shift_prev if kind == "prev" else shift))
                for s, (_, _, kind) in zip(logits, spans)
            ]
            total = functools.reduce(jnp.add, [jnp.sum(e, axis=1, keepdims=True) for e in expos])
            inverse = 1.0 / total
            result = None
            for e, (start, size, _) in zip(expos, spans):
                term = dot_f32((e * inverse).astype(jnp.bfloat16), value_head[start : start + size])
                result = term if result is None else result + term
            out_ref[part * half : (part + 1) * half, head * V_DIM : (head + 1) * V_DIM] = result.astype(jnp.bfloat16)
        peak_ref[0, head : head + 1, :] = jnp.broadcast_to(head_peak * SCALE, (1, 128))


def attend(seen, x, latents, rope, gathered, heads):
    pairs = heads // PAIR
    q_cols = heads * HEAD
    wide_q, wide_k = PAIR * HEAD, PAIR * QK_NOPE
    rows = gathered.shape[0]

    def weight(offset, width):
        return pl.BlockSpec((rows, width), lambda p: (0, offset // width + p))

    whole = lambda a: pl.BlockSpec(a.shape, lambda p: (0,) * a.ndim)
    k_at, v_at = 3 * q_cols, 3 * q_cols + heads * QK_NOPE
    return pl.pallas_call(
        attend_kernel,
        grid=(pairs,),
        in_specs=[
            pl.BlockSpec(memory_space=pltpu.SMEM),
            whole(x),
            whole(latents),
            whole(rope),
            weight(0, wide_q),
            weight(q_cols, wide_q),
            weight(2 * q_cols, wide_q),
            weight(k_at, wide_k),
            weight(v_at, wide_k),
        ],
        out_specs=[
            pl.BlockSpec((TOK, PAIR * V_DIM), lambda p: (0, p)),
            pl.BlockSpec((1, 8, 128), lambda p: (p, 0, 0)),
        ],
        out_shape=[
            jax.ShapeDtypeStruct((TOK, heads * V_DIM), jnp.bfloat16),
            jax.ShapeDtypeStruct((pairs, 8, 128), jnp.float32),
        ],
        compiler_params=pltpu.CompilerParams(vmem_limit_bytes=48 * 1024 * 1024),
        cost_estimate=pl.CostEstimate(flops=14_000_000_000, bytes_accessed=20_000_000, transcendentals=8_000_000),
    )(seen, x, latents, rope, gathered, gathered, gathered, gathered, gathered)


def local(query_latent, shared_latent, rope_keys, block_order, query_weight, key_weight, value_weight):
    heads = key_weight.shape[1] // QK_NOPE
    packed = jnp.concatenate(
        [query_weight[0:8], query_weight[8:16], query_weight[16:24], key_weight, value_weight], axis=1
    )
    gathered = lax.all_gather(packed, GATHER, axis=0, tiled=True)

    cycle = lax.axis_size("z") * lax.axis_size("xl")
    route = [(i, (i + 1) % cycle) for i in range(cycle)]
    lat_prev = lax.ppermute(shared_latent[0], ("z", "xl"), route)
    rope_prev = lax.ppermute(rope_keys[0], ("z", "xl"), route)
    latents = jnp.concatenate([shared_latent[0], lat_prev], axis=0)
    latents = latents.reshape(2 * TOK, 2, 2, 8, 2, 8).transpose(0, 3, 1, 4, 2, 5).reshape(2 * TOK, 512)
    rope = jnp.concatenate([rope_keys[0], rope_prev], axis=0)
    x = query_latent[0].reshape(TOK, 2, 2, 8, 2, 3, 8).transpose(5, 0, 3, 1, 4, 2, 6).reshape(3, TOK, 512)

    position = lax.axis_index(("z", "xl"))
    order_row = block_order[lax.axis_index(("xh", "core"))]
    seen = (order_row[(position - 1 + cycle) % cycle] < order_row[position]).astype(jnp.int32).reshape(1)

    attended, peaks = attend(seen, x, latents, rope, gathered, heads)
    peaks = peaks[:, :PAIR, 0].reshape(1, heads)
    everyone = math.prod(lax.axis_size(a) for a in GROUP)
    shared = lax.all_to_all(jnp.broadcast_to(peaks[None], (everyone, 1, heads)), GATHER, 0, 0)
    logit_max = jnp.max(shared, axis=(0, 1))
    clip = TAU / jnp.maximum(logit_max, TAU)
    root = jnp.sqrt(clip)
    factors = jnp.concatenate(
        [jnp.broadcast_to(root[:, None], (heads, QK_NOPE)), jnp.broadcast_to(clip[:, None], (heads, QK_ROPE))], axis=1
    ).reshape(1, heads * HEAD)
    clipped_q = (query_weight.astype(jnp.float32) * factors).astype(jnp.bfloat16)
    clipped_k = (key_weight.astype(jnp.float32) * jnp.repeat(root, QK_NOPE)[None]).astype(jnp.bfloat16)
    return (attended[None], logit_max, clipped_q, clipped_k)


def solution(mesh):
    fine = Mesh(mesh.devices.reshape(2, 2, 8, 2, 4), ("xh", "core", "z", "xl", "tensor"))
    dp, ctx = ("xh", "core"), ("z", "xl")
    return jax.shard_map(
        local,
        mesh=fine,
        in_specs=(
            P(dp, ctx, None),
            P(dp, ctx, None),
            P(dp, ctx, None),
            P(),
            P(GROUP, "tensor"),
            P(GROUP, "tensor"),
            P(GROUP, "tensor"),
        ),
        out_specs=(
            P(dp, ctx, "tensor"),
            P("tensor"),
            P(GROUP, "tensor"),
            P(GROUP, "tensor"),
        ),
        check_vma=False,
    )
```

```python
import functools
import math

import jax
import jax.numpy as jnp
from jax import lax
from jax.experimental import pallas as pl
from jax.experimental.pallas import tpu as pltpu
from jax.sharding import Mesh
from jax.sharding import PartitionSpec as P

QK_NOPE = 128
QK_ROPE = 64
V_DIM = 128
TAU = 100
HEAD = QK_NOPE + QK_ROPE
SCALE = 1.0 / math.sqrt(HEAD)
SCALE2 = SCALE * math.log2(math.e)
FAR = 1e30

GROUP = ("xh", "core", "z", "xl")
X = ("xh", "xl")
TOK = 512
HALF = TOK // 2
PAIR = 2
Q_WIDE = PAIR * HEAD
K_WIDE = PAIR * QK_NOPE
WIDE = 3 * Q_WIDE + 2 * K_WIDE
PAIRS = 8
PAIRS_A = 5
PAIRS_B = PAIRS - PAIRS_A
MIB = 1024 * 1024
VMEM = pl.BlockSpec(memory_space=pltpu.VMEM)
SMEM = pl.BlockSpec(memory_space=pltpu.SMEM)
ANY = pl.BlockSpec(memory_space=pl.ANY)


def dot_f32(a, b):
    return jnp.dot(a, b, preferred_element_type=jnp.float32)


def dot_t(a, b):
    return lax.dot_general(a, b, (((1,), (1,)), ((), ())), preferred_element_type=jnp.float32)


def attend_pair(seen, x_ref, lat_ref, rope_ref, weight, out_ref, peak_ref):
    query = functools.reduce(jnp.add, [dot_f32(x_ref[j], weight(j * Q_WIDE, Q_WIDE)) for j in range(3)])
    query = query.astype(jnp.bfloat16)
    keys = dot_f32(lat_ref[...], weight(3 * Q_WIDE, K_WIDE)).astype(jnp.bfloat16)
    values = dot_f32(lat_ref[...], weight(3 * Q_WIDE + K_WIDE, K_WIDE)).astype(jnp.bfloat16)
    rope = rope_ref[...]
    row = lax.broadcasted_iota(jnp.int32, (HALF, HALF), 0)
    col = lax.broadcasted_iota(jnp.int32, (HALF, HALF), 1)
    diagonal = col <= row
    ones = (lax.broadcasted_iota(jnp.int32, (2 * TOK, V_DIM), 1) == 0).astype(jnp.bfloat16)

    def logits_of(head, part):
        q_part = query[part * HALF : (part + 1) * HALF, head * HEAD : (head + 1) * HEAD]
        key_head = jnp.concatenate([keys[:, head * QK_NOPE : (head + 1) * QK_NOPE], rope], axis=1)
        spans = [(0, HALF, "all")] if part == 1 else []
        spans += [(part * HALF, HALF, "diag"), (TOK, TOK, "prev")]
        logits = []
        for start, size, kind in spans:
            s = dot_t(q_part, key_head[start : start + size])
            logits.append(jnp.where(diagonal, s, -jnp.inf) if kind == "diag" else s)
        return spans, logits

    def finish(head, part, spans, logits):
        value_head = jnp.concatenate([values[:, head * V_DIM : (head + 1) * V_DIM], ones], axis=1)
        peak = functools.reduce(jnp.maximum, [jnp.max(s, axis=1, keepdims=True) for s in logits[:-1]])
        prev_peak = jnp.max(logits[-1], axis=1, keepdims=True)
        peak = jnp.where(seen, jnp.maximum(peak, prev_peak), peak)
        shift = peak * SCALE2
        shift_prev = jnp.where(seen, shift, FAR)
        result = None
        for s, (start, size, kind) in zip(logits, spans):
            expo = jnp.exp2(s * SCALE2 - (shift_prev if kind == "prev" else shift))
            term = dot_f32(expo.astype(jnp.bfloat16), value_head[start : start + size])
            result = term if result is None else result + term
        result = result[:, :V_DIM] * (1.0 / result[:, V_DIM : V_DIM + 1])
        out_ref[part * HALF : (part + 1) * HALF, head * V_DIM : (head + 1) * V_DIM] = result.astype(jnp.bfloat16)
        return jnp.max(peak)

    order = [(head, part) for head in range(PAIR) for part in range(2)]
    peaks = []
    current = logits_of(*order[0])
    for i, (head, part) in enumerate(order):
        following = logits_of(*order[i + 1]) if i + 1 < len(order) else None
        peaks.append(finish(head, part, *current))
        current = following
    for head in range(PAIR):
        top = jnp.maximum(peaks[2 * head], peaks[2 * head + 1]) * SCALE
        peak_ref[0, head : head + 1, :] = jnp.broadcast_to(top, (1, 128))


def late_kernel(place_ref, x_ref, lat_ref, rope_ref, w_ref, _out, _peaks, out_ref, peak_ref):
    attend_pair(
        place_ref[0] > 0, x_ref, lat_ref, rope_ref, lambda start, width: w_ref[:, start : start + width], out_ref, peak_ref
    )


def early_kernel(place_ref, x_ref, lat_ref, rope_ref, *rest):
    pieces, (out_ref, peak_ref, w_ref, sems) = rest[:10], rest[10:]
    pair = pl.program_id(0)

    @pl.when(pair == 0)
    def _():
        me, core = place_ref[1], place_ref[2]
        copies = []
        for side in range(2):
            owner = core if side == 0 else 1 - core
            own, before, after, far_low, far_high = pieces[5 * side : 5 * side + 5]
            for piece, step, first in ((own, 0, 0), (before, 3, 0), (after, 1, 0), (far_low, 2, 0), (far_high, 2, 32)):
                block = lax.rem(me + step, 4) * 2 + owner
                rows = pl.ds(pl.multiple_of(block * 64 + first, 32), piece.shape[0])
                copies.append(pltpu.make_async_copy(piece, w_ref.at[rows, :], sems.at[len(copies)]))
        for copy in copies:
            copy.start()
        for copy in copies:
            copy.wait()

    def weight(start, width):
        return w_ref[:, pl.ds(pl.multiple_of(pair * WIDE + start, 128), width)]

    attend_pair(place_ref[0] > 0, x_ref, lat_ref, rope_ref, weight, out_ref, peak_ref)


def whole(array):
    return pl.BlockSpec(array.shape, lambda p: (0,) * array.ndim)


def cost(pairs):
    return pl.CostEstimate(flops=1_800_000_000 * pairs, bytes_accessed=2_000_000 * pairs, transcendentals=1_000_000 * pairs)


def outputs(first):
    specs = [
        pl.BlockSpec((TOK, PAIR * V_DIM), lambda p: (0, first + p)),
        pl.BlockSpec((1, 8, 128), lambda p: (first + p, 0, 0)),
    ]
    shapes = [
        jax.ShapeDtypeStruct((TOK, PAIRS * PAIR * V_DIM), jnp.bfloat16),
        jax.ShapeDtypeStruct((PAIRS, 8, 128), jnp.float32),
    ]
    return specs, shapes


def attend_early(place, x, latents, rope, pieces):
    specs, shapes = outputs(PAIRS_A)
    return pl.pallas_call(
        early_kernel,
        grid=(PAIRS_B,),
        in_specs=[SMEM, whole(x), whole(latents), whole(rope)] + [ANY] * len(pieces),
        out_specs=specs,
        out_shape=shapes,
        scratch_shapes=[
            pltpu.VMEM((TOK, PAIRS_B * WIDE), jnp.bfloat16),
            pltpu.SemaphoreType.DMA((len(pieces),)),
        ],
        compiler_params=pltpu.CompilerParams(vmem_limit_bytes=36 * MIB),
        cost_estimate=cost(PAIRS_B),
        name="early",
    )(place, x, latents, rope, *pieces)


def attend_late(place, x, latents, rope, gathered, out, peaks):
    specs, shapes = outputs(0)
    return pl.pallas_call(
        late_kernel,
        grid=(PAIRS_A,),
        in_specs=[SMEM, whole(x), whole(latents), whole(rope)]
        + [pl.BlockSpec((TOK, WIDE), lambda p: (0, p)), ANY, ANY],
        out_specs=specs,
        out_shape=shapes,
        input_output_aliases={5: 0, 6: 1},
        compiler_params=pltpu.CompilerParams(vmem_limit_bytes=56 * MIB),
        cost_estimate=cost(PAIRS_A),
        name="late",
    )(place, x, latents, rope, gathered, out, peaks)


def pack_kernel(q_ref, k_ref, v_ref, a_ref, b_ref):
    for pair in range(PAIRS):
        ref, at = (a_ref, pair) if pair < PAIRS_A else (b_ref, pair - PAIRS_A)
        at = at * WIDE
        for j in range(3):
            ref[:, at + j * Q_WIDE : at + (j + 1) * Q_WIDE] = q_ref[8 * j : 8 * j + 8, pair * Q_WIDE : (pair + 1) * Q_WIDE]
        at += 3 * Q_WIDE
        ref[:, at : at + K_WIDE] = k_ref[:, pair * K_WIDE : (pair + 1) * K_WIDE]
        ref[:, at + K_WIDE : at + 2 * K_WIDE] = v_ref[:, pair * K_WIDE : (pair + 1) * K_WIDE]


def pack(query_weight, key_weight, value_weight):
    return pl.pallas_call(
        pack_kernel,
        in_specs=[VMEM] * 3,
        out_specs=[VMEM] * 2,
        out_shape=[
            jax.ShapeDtypeStruct((8, PAIRS_A * WIDE), jnp.bfloat16),
            jax.ShapeDtypeStruct((8, PAIRS_B * WIDE), jnp.bfloat16),
        ],
        name="pack",
    )(query_weight, key_weight, value_weight)


def order_kernel(offsets, me_ref, *refs):
    pieces, out_ref, stack = refs[:-2], refs[-2], refs[-1]
    count = len(pieces)
    for offset, piece in zip(offsets, pieces):
        stack[offset % count] = piece[...]
    me = me_ref[0]
    for slot in range(0, count, 2):
        two = [stack[lax.rem(slot + i + count - me, count)] for i in range(2)]
        out_ref[8 * slot : 8 * slot + 16, :] = jnp.concatenate(two, axis=0)


def in_order(me, offsets, pieces):
    rows, columns = pieces[0].shape
    count = len(pieces)
    return pl.pallas_call(
        functools.partial(order_kernel, offsets),
        in_specs=[SMEM] + [VMEM] * count,
        out_specs=VMEM,
        out_shape=jax.ShapeDtypeStruct((rows * count, columns), jnp.bfloat16),
        scratch_shapes=[pltpu.VMEM((count, rows, columns), jnp.bfloat16)],
        name="in_order",
    )(me.reshape(1), *pieces)


def moved(block, axes, distance):
    count = lax.axis_size(axes)
    return lax.ppermute(block, axes, [(i, (i + distance) % count) for i in range(count)])


def local(query_latent, shared_latent, rope_keys, block_order, query_weight, key_weight, value_weight):
    heads = key_weight.shape[1] // QK_NOPE
    me_x = lax.axis_index(X).astype(jnp.int32)
    me_z = lax.axis_index("z").astype(jnp.int32)
    me_core = lax.axis_index("core").astype(jnp.int32)
    cycle = lax.axis_size(("z", "xl"))
    position = lax.axis_index(("z", "xl"))
    order_row = block_order[lax.axis_index(("xh", "core"))]
    seen = (order_row[(position - 1 + cycle) % cycle] < order_row[position]).astype(jnp.int32)
    place = jnp.stack([seen, me_x, me_core])

    packed_a, packed_b = pack(query_weight, key_weight, value_weight)

    along_x = [packed_a, moved(packed_a, X, 1), moved(packed_a, X, -1), moved(packed_a, X, 2)]
    shard_a = in_order(me_x, (0, -1, 1, 2), along_x)
    gathered_a = lax.all_gather(shard_a, ("z", "core"), axis=0, tiled=True)

    along_z, offsets = [packed_b], [0]
    up = down = packed_b
    for step in range(1, 5):
        up = moved(up, "z", 1)
        along_z.append(up)
        offsets.append(-step)
        if step < 4:
            down = moved(down, "z", -1)
            along_z.append(down)
            offsets.append(step)
    own = in_order(me_z, tuple(offsets), along_z)
    before, after = moved(own, X, 1), moved(own, X, -1)
    far_low, far_high = moved(before[:32], X, 1), moved(after[32:], X, -1)
    mine = [own, before, after, far_low, far_high]
    pieces = mine + [moved(piece, "core", 1) for piece in mine]

    lat_prev = moved(shared_latent[0], ("z", "xl"), 1)
    rope_prev = moved(rope_keys[0], ("z", "xl"), 1)
    latents = jnp.concatenate([shared_latent[0], lat_prev], axis=0).reshape(2 * TOK, 2, 2, 8, 2, 8)
    rope = jnp.concatenate([rope_keys[0], rope_prev], axis=0)
    x = query_latent[0].reshape(TOK, 2, 2, 8, 2, 3, 8)
    lat_a = latents.transpose(0, 3, 2, 1, 4, 5).reshape(2 * TOK, 512)
    lat_b = latents.transpose(0, 1, 4, 2, 3, 5).reshape(2 * TOK, 512)
    x_a = x.transpose(5, 0, 3, 2, 1, 4, 6).reshape(3, TOK, 512)
    x_b = x.transpose(5, 0, 1, 4, 2, 3, 6).reshape(3, TOK, 512)

    attended, peaks = attend_early(place, x_b, lat_b, rope, pieces)
    attended, peaks = attend_late(place, x_a, lat_a, rope, gathered_a, attended, peaks)

    peaks = peaks[:, :PAIR, 0].reshape(1, heads)
    everyone = lax.axis_size(GROUP)
    shared = lax.all_to_all(jnp.broadcast_to(peaks[None], (everyone, 1, heads)), GROUP, 0, 0)
    logit_max = jnp.max(shared, axis=(0, 1))
    clip = TAU / jnp.maximum(logit_max, TAU)
    root = jnp.sqrt(clip)
    factors = jnp.concatenate(
        [jnp.broadcast_to(root[:, None], (heads, QK_NOPE)), jnp.broadcast_to(clip[:, None], (heads, QK_ROPE))], axis=1
    ).reshape(1, heads * HEAD)
    clipped_q = (query_weight.astype(jnp.float32) * factors).astype(jnp.bfloat16)
    clipped_k = (key_weight.astype(jnp.float32) * jnp.repeat(root, QK_NOPE)[None]).astype(jnp.bfloat16)
    return (attended[None], logit_max, clipped_q, clipped_k)


def solution(mesh):
    fine = Mesh(mesh.devices.reshape(2, 2, 8, 2, 4), ("xh", "core", "z", "xl", "tensor"))
    dp, ctx = ("xh", "core"), ("z", "xl")
    return jax.shard_map(
        local,
        mesh=fine,
        in_specs=(
            P(dp, ctx, None),
            P(dp, ctx, None),
            P(dp, ctx, None),
            P(),
            P(GROUP, "tensor"),
            P(GROUP, "tensor"),
            P(GROUP, "tensor"),
        ),
        out_specs=(
            P(dp, ctx, "tensor"),
            P("tensor"),
            P(GROUP, "tensor"),
            P(GROUP, "tensor"),
        ),
        check_vma=False,
    )
```

```python
import functools
import math

import jax
import jax.numpy as jnp
from jax import lax
from jax.experimental import pallas as pl
from jax.experimental.pallas import tpu as pltpu
from jax.sharding import Mesh
from jax.sharding import PartitionSpec as P

QK_NOPE = 128
QK_ROPE = 64
V_DIM = 128
TAU = 100
HEAD = QK_NOPE + QK_ROPE
SCALE = 1.0 / math.sqrt(HEAD)
SCALE2 = SCALE * math.log2(math.e)
FAR = 1e30

GROUP = ("xh", "core", "z", "xl")
X = ("xh", "xl")
TOK = 512
HALF = TOK // 2
PAIR = 2
Q_WIDE = PAIR * HEAD
K_WIDE = PAIR * QK_NOPE
WIDE = 3 * Q_WIDE + 2 * K_WIDE
PAIRS = 8
PAIRS_A = 5
PAIRS_B = PAIRS - PAIRS_A
MIB = 1024 * 1024
VMEM = pl.BlockSpec(memory_space=pltpu.VMEM)
SMEM = pl.BlockSpec(memory_space=pltpu.SMEM)
ANY = pl.BlockSpec(memory_space=pl.ANY)


def dot_f32(a, b):
    return jnp.dot(a, b, preferred_element_type=jnp.float32)


def dot_t(a, b):
    return lax.dot_general(a, b, (((1,), (1,)), ((), ())), preferred_element_type=jnp.float32)


def attend_pair(seen, x_ref, lat_ref, rope_ref, weight, out_ref, peak_ref):
    query = functools.reduce(jnp.add, [dot_f32(x_ref[j], weight(j * Q_WIDE, Q_WIDE)) for j in range(3)])
    query = query.astype(jnp.bfloat16)
    keys = dot_f32(lat_ref[...], weight(3 * Q_WIDE, K_WIDE)).astype(jnp.bfloat16)
    values = dot_f32(lat_ref[...], weight(3 * Q_WIDE + K_WIDE, K_WIDE)).astype(jnp.bfloat16)
    rope = rope_ref[...]
    row = lax.broadcasted_iota(jnp.int32, (HALF, HALF), 0)
    col = lax.broadcasted_iota(jnp.int32, (HALF, HALF), 1)
    diagonal = col <= row
    ones = (lax.broadcasted_iota(jnp.int32, (2 * TOK, V_DIM), 1) == 0).astype(jnp.bfloat16)

    def logits_of(head, part):
        q_part = query[part * HALF : (part + 1) * HALF, head * HEAD : (head + 1) * HEAD]
        key_head = jnp.concatenate([keys[:, head * QK_NOPE : (head + 1) * QK_NOPE], rope], axis=1)
        spans = [(0, HALF, "all")] if part == 1 else []
        spans += [(part * HALF, HALF, "diag"), (TOK, TOK, "prev")]
        logits = []
        for start, size, kind in spans:
            s = dot_t(q_part, key_head[start : start + size])
            logits.append(jnp.where(diagonal, s, -jnp.inf) if kind == "diag" else s)
        return spans, logits

    def finish(head, part, spans, logits):
        value_head = jnp.concatenate([values[:, head * V_DIM : (head + 1) * V_DIM], ones], axis=1)
        peak = functools.reduce(jnp.maximum, [jnp.max(s, axis=1, keepdims=True) for s in logits[:-1]])
        prev_peak = jnp.max(logits[-1], axis=1, keepdims=True)
        peak = jnp.where(seen, jnp.maximum(peak, prev_peak), peak)
        shift = peak * SCALE2
        shift_prev = jnp.where(seen, shift, FAR)
        result = None
        for s, (start, size, kind) in zip(logits, spans):
            expo = jnp.exp2(s * SCALE2 - (shift_prev if kind == "prev" else shift))
            term = dot_f32(expo.astype(jnp.bfloat16), value_head[start : start + size])
            result = term if result is None else result + term
        result = result[:, :V_DIM] * (1.0 / result[:, V_DIM : V_DIM + 1])
        out_ref[part * HALF : (part + 1) * HALF, head * V_DIM : (head + 1) * V_DIM] = result.astype(jnp.bfloat16)
        return jnp.max(peak)

    order = [(head, part) for head in range(PAIR) for part in range(2)]
    peaks = []
    current = logits_of(*order[0])
    for i, (head, part) in enumerate(order):
        following = logits_of(*order[i + 1]) if i + 1 < len(order) else None
        peaks.append(finish(head, part, *current))
        current = following
    for head in range(PAIR):
        top = jnp.maximum(peaks[2 * head], peaks[2 * head + 1]) * SCALE
        peak_ref[0, head : head + 1, :] = jnp.broadcast_to(top, (1, 128))


def late_kernel(place_ref, x_ref, lat_ref, rope_ref, w_ref, _out, _peaks, out_ref, peak_ref):
    attend_pair(
        place_ref[0] > 0, x_ref, lat_ref, rope_ref, lambda start, width: w_ref[:, start : start + width], out_ref, peak_ref
    )


def early_kernel(place_ref, x_ref, lat_ref, rope_ref, *rest):
    pieces, (out_ref, peak_ref, w_ref, sems) = rest[:10], rest[10:]
    pair = pl.program_id(0)

    @pl.when(pair == 0)
    def _():
        me, core = place_ref[1], place_ref[2]
        copies = []
        for side in range(2):
            owner = core if side == 0 else 1 - core
            own, before, after, far_low, far_high = pieces[5 * side : 5 * side + 5]
            for piece, step, first in ((own, 0, 0), (before, 3, 0), (after, 1, 0), (far_low, 2, 0), (far_high, 2, 32)):
                block = lax.rem(me + step, 4) * 2 + owner
                rows = pl.ds(pl.multiple_of(block * 64 + first, 32), piece.shape[0])
                copies.append(pltpu.make_async_copy(piece, w_ref.at[rows, :], sems.at[len(copies)]))
        for copy in copies:
            copy.start()
        for copy in copies:
            copy.wait()

    def weight(start, width):
        return w_ref[:, pl.ds(pl.multiple_of(pair * WIDE + start, 128), width)]

    attend_pair(place_ref[0] > 0, x_ref, lat_ref, rope_ref, weight, out_ref, peak_ref)


def whole(array):
    return pl.BlockSpec(array.shape, lambda p: (0,) * array.ndim)


def cost(pairs):
    return pl.CostEstimate(flops=1_800_000_000 * pairs, bytes_accessed=2_000_000 * pairs, transcendentals=1_000_000 * pairs)


def outputs(first):
    specs = [
        pl.BlockSpec((TOK, PAIR * V_DIM), lambda p: (0, first + p)),
        pl.BlockSpec((1, 8, 128), lambda p: (first + p, 0, 0)),
    ]
    shapes = [
        jax.ShapeDtypeStruct((TOK, PAIRS * PAIR * V_DIM), jnp.bfloat16),
        jax.ShapeDtypeStruct((PAIRS, 8, 128), jnp.float32),
    ]
    return specs, shapes


def attend_early(place, x, latents, rope, pieces):
    specs, shapes = outputs(PAIRS_A)
    return pl.pallas_call(
        early_kernel,
        grid=(PAIRS_B,),
        in_specs=[SMEM, whole(x), whole(latents), whole(rope)] + [ANY] * len(pieces),
        out_specs=specs,
        out_shape=shapes,
        scratch_shapes=[
            pltpu.VMEM((TOK, PAIRS_B * WIDE), jnp.bfloat16),
            pltpu.SemaphoreType.DMA((len(pieces),)),
        ],
        compiler_params=pltpu.CompilerParams(vmem_limit_bytes=36 * MIB),
        cost_estimate=cost(PAIRS_B),
        name="early",
    )(place, x, latents, rope, *pieces)


def attend_late(place, x, latents, rope, gathered, out, peaks):
    specs, shapes = outputs(0)
    return pl.pallas_call(
        late_kernel,
        grid=(PAIRS_A,),
        in_specs=[SMEM, whole(x), whole(latents), whole(rope)]
        + [pl.BlockSpec((TOK, WIDE), lambda p: (0, p)), ANY, ANY],
        out_specs=specs,
        out_shape=shapes,
        input_output_aliases={5: 0, 6: 1},
        compiler_params=pltpu.CompilerParams(vmem_limit_bytes=56 * MIB),
        cost_estimate=cost(PAIRS_A),
        name="late",
    )(place, x, latents, rope, gathered, out, peaks)


def pack_kernel(q_ref, k_ref, v_ref, a_ref, b_ref):
    for pair in range(PAIRS):
        ref, at = (a_ref, pair) if pair < PAIRS_A else (b_ref, pair - PAIRS_A)
        at = at * WIDE
        for j in range(3):
            ref[:, at + j * Q_WIDE : at + (j + 1) * Q_WIDE] = q_ref[8 * j : 8 * j + 8, pair * Q_WIDE : (pair + 1) * Q_WIDE]
        at += 3 * Q_WIDE
        ref[:, at : at + K_WIDE] = k_ref[:, pair * K_WIDE : (pair + 1) * K_WIDE]
        ref[:, at + K_WIDE : at + 2 * K_WIDE] = v_ref[:, pair * K_WIDE : (pair + 1) * K_WIDE]


def pack(query_weight, key_weight, value_weight):
    return pl.pallas_call(
        pack_kernel,
        in_specs=[VMEM] * 3,
        out_specs=[VMEM] * 2,
        out_shape=[
            jax.ShapeDtypeStruct((8, PAIRS_A * WIDE), jnp.bfloat16),
            jax.ShapeDtypeStruct((8, PAIRS_B * WIDE), jnp.bfloat16),
        ],
        name="pack",
    )(query_weight, key_weight, value_weight)


def order_kernel(offsets, me_ref, *refs):
    pieces, out_ref = refs[:-1], refs[-1]
    count = len(pieces)
    for offset, piece in zip(offsets, pieces):
        out_ref[lax.rem(me_ref[0] + offset % count, count)] = piece[...]


def in_order(me, offsets, pieces):
    rows, columns = pieces[0].shape
    count = len(pieces)
    return pl.pallas_call(
        functools.partial(order_kernel, offsets),
        in_specs=[SMEM] + [VMEM] * count,
        out_specs=VMEM,
        out_shape=jax.ShapeDtypeStruct((count, rows, columns), jnp.bfloat16),
        name="in_order",
    )(me.reshape(1), *pieces).reshape(count * rows, columns)


def one_hot(source, first):
    at = lax.broadcasted_iota(jnp.int32, (128, source.shape[1]), 0) + first
    return jnp.where(at == source, 1.0, 0.0).astype(jnp.bfloat16)


def picked(rows, tiles, source):
    left = jnp.concatenate([rows(tile) for tile in tiles], axis=1)
    right = jnp.concatenate([one_hot(source, tile * 128) for tile in tiles], axis=0)
    return dot_f32(left, right).astype(jnp.bfloat16)


def late_source(c, tile, strip):
    z, core, xh, xl, r = 2 * tile + ((c >> 6) & 1), (c >> 5) & 1, (c >> 4) & 1, (c >> 3) & 1, c & 7
    return ((xh * 2 + core) * 16 + z * 2 + xl) * strip + r


def early_source(c, tile, strip):
    core, z, r = (c >> 6) & 1, (c >> 3) & 7, c & 7
    return ((tile // 2 * 2 + core) * 16 + z * 2 + tile % 2) * strip + r


def order_query_kernel(x_ref, late_ref, early_ref):
    column = lax.broadcasted_iota(jnp.int32, (1, 384), 1)
    c, j = column & 127, column >> 7
    rows = lambda tile: x_ref[:, tile * 128 : (tile + 1) * 128]
    for tile in range(4):
        low, high = 96 * tile // 128, (96 * tile + 95) // 128
        near = [3 * block + part for block in range(4) for part in range(low, high + 1)]
        late = picked(rows, near, late_source(c, tile, 24) + 8 * j)
        near = [3 * (tile // 2 * 2 + core) + part for core in range(2) for part in range(3)]
        early = picked(rows, near, early_source(c, tile, 24) + 8 * j)
        for strip in range(3):
            late_ref[strip, :, tile * 128 : (tile + 1) * 128] = late[:, strip * 128 : (strip + 1) * 128]
            early_ref[strip, :, tile * 128 : (tile + 1) * 128] = early[:, strip * 128 : (strip + 1) * 128]


def order_query(x):
    shape = jax.ShapeDtypeStruct((3, TOK, 512), jnp.bfloat16)
    return pl.pallas_call(
        order_query_kernel,
        in_specs=[VMEM],
        out_specs=[VMEM] * 2,
        out_shape=[shape, shape],
        compiler_params=pltpu.CompilerParams(vmem_limit_bytes=24 * MIB),
        cost_estimate=pl.CostEstimate(flops=2_500_000_000, bytes_accessed=6_000_000, transcendentals=0),
        name="order_query",
    )(x)


def order_latent_kernel(me_ref, own_ref, own_rope_ref, *refs):
    pieces, (late_ref, early_ref, rope_ref, prev_ref) = refs[:4], refs[4:]
    for offset, piece in zip((0, -1, 1, 2), pieces):
        slot = lax.rem(me_ref[0] + offset % 4, 4)
        prev_ref[pl.ds(pl.multiple_of(slot * 128, 128), 128), :] = piece[...]
    rope_ref[:TOK] = own_rope_ref[...]
    rope_ref[TOK:] = prev_ref[:, 512:]
    c = lax.broadcasted_iota(jnp.int32, (1, 128), 1)
    for part, ref in ((0, own_ref), (1, prev_ref)):
        rows = lambda tile: ref[:, tile * 128 : (tile + 1) * 128]
        for tile in range(4):
            at = slice(tile * 128, (tile + 1) * 128)
            late_ref[part * TOK : (part + 1) * TOK, at] = picked(rows, range(4), late_source(c, tile, 8))
            near = [tile // 2 * 2, tile // 2 * 2 + 1]
            early_ref[part * TOK : (part + 1) * TOK, at] = picked(rows, near, early_source(c, tile, 8))


def order_latent(me, own, own_rope, pieces):
    shape = jax.ShapeDtypeStruct((2 * TOK, 512), jnp.bfloat16)
    return pl.pallas_call(
        order_latent_kernel,
        in_specs=[SMEM] + [VMEM] * 6,
        out_specs=[VMEM] * 3,
        out_shape=[shape, shape, jax.ShapeDtypeStruct((2 * TOK, QK_ROPE), jnp.bfloat16)],
        scratch_shapes=[pltpu.VMEM((TOK, 512 + QK_ROPE), jnp.bfloat16)],
        compiler_params=pltpu.CompilerParams(vmem_limit_bytes=24 * MIB),
        cost_estimate=pl.CostEstimate(flops=1_000_000_000, bytes_accessed=4_000_000, transcendentals=0),
        name="order_latent",
    )(me.reshape(1), own, own_rope, *pieces)


def moved(block, axes, distance):
    count = lax.axis_size(axes)
    return lax.ppermute(block, axes, [(i, (i + distance) % count) for i in range(count)])


def local(query_latent, shared_latent, rope_keys, block_order, query_weight, key_weight, value_weight):
    heads = key_weight.shape[1] // QK_NOPE
    me_x = lax.axis_index(X).astype(jnp.int32)
    me_z = lax.axis_index("z").astype(jnp.int32)
    me_core = lax.axis_index("core").astype(jnp.int32)
    cycle = lax.axis_size(("z", "xl"))
    position = lax.axis_index(("z", "xl"))
    order_row = block_order[lax.axis_index(("xh", "core"))]
    seen = (order_row[(position - 1 + cycle) % cycle] < order_row[position]).astype(jnp.int32)
    place = jnp.stack([seen, me_x, me_core])

    packed_a, packed_b = pack(query_weight, key_weight, value_weight)

    barrier = lax.optimization_barrier
    me_t = lax.axis_index("tensor").astype(jnp.int32)
    quarter = TOK // lax.axis_size("tensor")
    latent, rope_own = shared_latent[0], rope_keys[0]

    along_x = [packed_a, moved(packed_a, X, 1), moved(packed_a, X, -1), moved(packed_a, X, 2)]
    shard_a = in_order(me_x, (0, -1, 1, 2), along_x)
    mine = jnp.concatenate(
        [lax.dynamic_slice_in_dim(a, me_t * quarter, quarter, 0) for a in (latent, rope_own)], axis=1
    )
    shard_a, mine, packed_b = barrier((shard_a, mine, packed_b))
    gathered_a = lax.all_gather(shard_a, ("z", "core"), axis=0, tiled=True)

    up, down = moved(packed_b, "z", 1), moved(packed_b, "z", -1)
    up2, down2 = moved(packed_b, "z", 2), moved(packed_b, "z", -2)
    up3, down3, up4 = moved(up, "z", 2), moved(down, "z", -2), moved(up2, "z", 2)
    own = in_order(me_z, (0, -1, 1, -2, 2, -3, 3, -4), [packed_b, up, down, up2, down2, up3, down3, up4])
    theirs = moved(mine, ("z", "xl"), 1)
    own, theirs = barrier((own, theirs))

    before, after = moved(own, X, 1), moved(own, X, -1)
    prev = [theirs, moved(theirs, "tensor", 1), moved(theirs, "tensor", -1), moved(theirs, "tensor", 2)]
    x_a, x_b = order_query(query_latent[0])
    before, after, x_a, x_b = barrier((before, after, x_a, x_b))
    far_low, far_high = moved(before[:32], X, 1), moved(after[32:], X, -1)
    lat_a, lat_b, rope = order_latent(me_t, latent, rope_own, prev)
    far_low, far_high, lat_a, lat_b, rope = barrier((far_low, far_high, lat_a, lat_b, rope))
    mine = [own, before, after, far_low, far_high]
    pieces = mine + [moved(piece, "core", 1) for piece in mine]

    attended, peaks = attend_early(place, x_b, lat_b, rope, pieces)
    attended, peaks = attend_late(place, x_a, lat_a, rope, gathered_a, attended, peaks)

    peaks = peaks[:, :PAIR, 0].reshape(1, heads)
    everyone = lax.axis_size(GROUP)
    shared = lax.all_to_all(jnp.broadcast_to(peaks[None], (everyone, 1, heads)), GROUP, 0, 0)
    logit_max = jnp.max(shared, axis=(0, 1))
    clip = TAU / jnp.maximum(logit_max, TAU)
    root = jnp.sqrt(clip)
    factors = jnp.concatenate(
        [jnp.broadcast_to(root[:, None], (heads, QK_NOPE)), jnp.broadcast_to(clip[:, None], (heads, QK_ROPE))], axis=1
    ).reshape(1, heads * HEAD)
    clipped_q = (query_weight.astype(jnp.float32) * factors).astype(jnp.bfloat16)
    clipped_k = (key_weight.astype(jnp.float32) * jnp.repeat(root, QK_NOPE)[None]).astype(jnp.bfloat16)
    return (attended[None], logit_max, clipped_q, clipped_k)


def solution(mesh):
    fine = Mesh(mesh.devices.reshape(2, 2, 8, 2, 4), ("xh", "core", "z", "xl", "tensor"))
    dp, ctx = ("xh", "core"), ("z", "xl")
    return jax.shard_map(
        local,
        mesh=fine,
        in_specs=(
            P(dp, ctx, None),
            P(dp, ctx, None),
            P(dp, ctx, None),
            P(),
            P(GROUP, "tensor"),
            P(GROUP, "tensor"),
            P(GROUP, "tensor"),
        ),
        out_specs=(
            P(dp, ctx, "tensor"),
            P("tensor"),
            P(GROUP, "tensor"),
            P(GROUP, "tensor"),
        ),
        check_vma=False,
    )
```

```python
import functools
import math

import jax
import jax.numpy as jnp
from jax import lax
from jax.experimental import pallas as pl
from jax.experimental.pallas import tpu as pltpu
from jax.sharding import Mesh
from jax.sharding import PartitionSpec as P

QK_NOPE = 128
QK_ROPE = 64
V_DIM = 128
TAU = 100
HEAD = QK_NOPE + QK_ROPE
SCALE = 1.0 / math.sqrt(HEAD)
SCALE2 = SCALE * math.log2(math.e)
FAR = 1e30

GROUP = ("xh", "core", "z", "xl")
X = ("xh", "xl")
TOK = 512
HALF = TOK // 2
PAIR = 2
Q_WIDE = PAIR * HEAD
K_WIDE = PAIR * QK_NOPE
WIDE = 3 * Q_WIDE + 2 * K_WIDE
PAIRS = 8
PAIRS_A = 5
PAIRS_B = PAIRS - PAIRS_A
MIB = 1024 * 1024
VMEM = pl.BlockSpec(memory_space=pltpu.VMEM)
SMEM = pl.BlockSpec(memory_space=pltpu.SMEM)
ANY = pl.BlockSpec(memory_space=pl.ANY)
HBM = pl.BlockSpec(memory_space=pltpu.HBM)
EARLY_MIB = 24
LATE_MIB = 48


def dot_f32(a, b):
    return jnp.dot(a, b, preferred_element_type=jnp.float32)


def dot_t(a, b):
    return lax.dot_general(a, b, (((1,), (1,)), ((), ())), preferred_element_type=jnp.float32)


def attend_pair(seen, x_ref, lat_ref, rope_ref, weight, out_ref, peak_ref):
    query = functools.reduce(jnp.add, [dot_f32(x_ref[j], weight(j * Q_WIDE, Q_WIDE)) for j in range(3)])
    query = query.astype(jnp.bfloat16)
    keys = dot_f32(lat_ref[...], weight(3 * Q_WIDE, K_WIDE)).astype(jnp.bfloat16)
    values = dot_f32(lat_ref[...], weight(3 * Q_WIDE + K_WIDE, K_WIDE)).astype(jnp.bfloat16)
    rope = rope_ref[...]
    row = lax.broadcasted_iota(jnp.int32, (HALF, HALF), 0)
    col = lax.broadcasted_iota(jnp.int32, (HALF, HALF), 1)
    diagonal = col <= row
    ones = (lax.broadcasted_iota(jnp.int32, (2 * TOK, V_DIM), 1) == 0).astype(jnp.bfloat16)

    def logits_of(head, part):
        q_part = query[part * HALF : (part + 1) * HALF, head * HEAD : (head + 1) * HEAD]
        key_head = jnp.concatenate([keys[:, head * QK_NOPE : (head + 1) * QK_NOPE], rope], axis=1)
        spans = [(0, HALF, "all")] if part == 1 else []
        spans += [(part * HALF, HALF, "diag"), (TOK, TOK, "prev")]
        logits = []
        for start, size, kind in spans:
            s = dot_t(q_part, key_head[start : start + size])
            logits.append(jnp.where(diagonal, s, -jnp.inf) if kind == "diag" else s)
        return spans, logits

    def finish(head, part, spans, logits):
        value_head = jnp.concatenate([values[:, head * V_DIM : (head + 1) * V_DIM], ones], axis=1)
        peak = functools.reduce(jnp.maximum, [jnp.max(s, axis=1, keepdims=True) for s in logits[:-1]])
        prev_peak = jnp.max(logits[-1], axis=1, keepdims=True)
        peak = jnp.where(seen, jnp.maximum(peak, prev_peak), peak)
        shift = peak * SCALE2
        shift_prev = jnp.where(seen, shift, FAR)
        result = None
        for s, (start, size, kind) in zip(logits, spans):
            expo = jnp.exp2(s * SCALE2 - (shift_prev if kind == "prev" else shift))
            term = dot_f32(expo.astype(jnp.bfloat16), value_head[start : start + size])
            result = term if result is None else result + term
        result = result[:, :V_DIM] * (1.0 / result[:, V_DIM : V_DIM + 1])
        out_ref[part * HALF : (part + 1) * HALF, head * V_DIM : (head + 1) * V_DIM] = result.astype(jnp.bfloat16)
        return jnp.max(peak)

    order = [(head, part) for head in range(PAIR) for part in range(2)]
    peaks = []
    current = logits_of(*order[0])
    for i, (head, part) in enumerate(order):
        following = logits_of(*order[i + 1]) if i + 1 < len(order) else None
        peaks.append(finish(head, part, *current))
        current = following
    for head in range(PAIR):
        top = jnp.maximum(peaks[2 * head], peaks[2 * head + 1]) * SCALE
        peak_ref[0, head : head + 1, :] = jnp.broadcast_to(top, (1, 128))


def in_slots(pairs, copies, w_ref, sems):
    pair = pl.program_id(0)
    slot = lax.rem(pair, 2)

    @pl.when(pair == 0)
    def _():
        for copy in copies(0, 0):
            copy.start()

    @pl.when(pair + 1 < pairs)
    def _():
        for copy in copies(pair + 1, 1 - slot):
            copy.start()

    for copy in copies(pair, slot):
        copy.wait()
    return lambda start, width: w_ref[slot, :, start : start + width]


def late_kernel(place_ref, x_ref, lat_ref, rope_ref, all_ref, *rest):
    out_ref, peak_ref, w_ref, sems = rest[-4:]

    def copies(pair, slot):
        columns = pl.ds(pl.multiple_of(pair * WIDE, 128), WIDE)
        return [pltpu.make_async_copy(all_ref.at[:, columns], w_ref.at[slot], sems.at[slot, 0])]

    weight = in_slots(PAIRS_A, copies, w_ref, sems)
    attend_pair(place_ref[0] > 0, x_ref, lat_ref, rope_ref, weight, out_ref, peak_ref)


def early_kernel(place_ref, x_ref, lat_ref, rope_ref, *rest):
    pieces, (out_ref, peak_ref, w_ref, sems) = rest[:10], rest[-4:]
    me, core = place_ref[1], place_ref[2]

    def copies(pair, slot):
        columns = pl.ds(pl.multiple_of(pair * WIDE, 128), WIDE)
        made = []
        for side in range(2):
            owner = core if side == 0 else 1 - core
            for piece, step, first in zip(pieces[5 * side : 5 * side + 5], (0, 3, 1, 2, 2), (0, 0, 0, 0, 32)):
                block = lax.rem(me + step, 4) * 2 + owner
                rows = pl.ds(pl.multiple_of(block * 64 + first, 32), piece.shape[0])
                made.append(
                    pltpu.make_async_copy(piece.at[:, columns], w_ref.at[slot, rows, :], sems.at[slot, len(made)])
                )
        return made

    weight = in_slots(PAIRS_B, copies, w_ref, sems)
    attend_pair(place_ref[0] > 0, x_ref, lat_ref, rope_ref, weight, out_ref, peak_ref)


def attend(kernel, name, first, pairs, copies, place, x, latents, rope, weights, before=()):
    return pl.pallas_call(
        kernel,
        grid=(pairs,),
        in_specs=[SMEM, VMEM, VMEM, VMEM] + [HBM if len(weights) == 1 else ANY] * len(weights) + [ANY] * len(before),
        out_specs=[
            pl.BlockSpec((TOK, PAIR * V_DIM), lambda p: (0, first + p)),
            pl.BlockSpec((1, 8, 128), lambda p: (first + p, 0, 0)),
        ],
        out_shape=[
            jax.ShapeDtypeStruct((TOK, PAIRS * PAIR * V_DIM), jnp.bfloat16),
            jax.ShapeDtypeStruct((PAIRS, 8, 128), jnp.float32),
        ],
        input_output_aliases={4 + len(weights) + i: i for i in range(len(before))},
        scratch_shapes=[
            pltpu.VMEM((2, TOK, WIDE), jnp.bfloat16),
            pltpu.SemaphoreType.DMA((2, copies)),
        ],
        compiler_params=pltpu.CompilerParams(vmem_limit_bytes=(LATE_MIB if before else EARLY_MIB) * MIB),
        cost_estimate=pl.CostEstimate(
            flops=1_800_000_000 * pairs, bytes_accessed=2_000_000 * pairs, transcendentals=1_000_000 * pairs
        ),
        name=name,
    )(place, x, latents, rope, *weights, *before)


def pack_kernel(q_ref, k_ref, v_ref, a_ref, b_ref):
    for pair in range(PAIRS):
        ref, at = (a_ref, pair) if pair < PAIRS_A else (b_ref, pair - PAIRS_A)
        at = at * WIDE
        for j in range(3):
            ref[:, at + j * Q_WIDE : at + (j + 1) * Q_WIDE] = q_ref[8 * j : 8 * j + 8, pair * Q_WIDE : (pair + 1) * Q_WIDE]
        at += 3 * Q_WIDE
        ref[:, at : at + K_WIDE] = k_ref[:, pair * K_WIDE : (pair + 1) * K_WIDE]
        ref[:, at + K_WIDE : at + 2 * K_WIDE] = v_ref[:, pair * K_WIDE : (pair + 1) * K_WIDE]


def pack(query_weight, key_weight, value_weight):
    return pl.pallas_call(
        pack_kernel,
        in_specs=[VMEM] * 3,
        out_specs=[VMEM] * 2,
        out_shape=[
            jax.ShapeDtypeStruct((8, PAIRS_A * WIDE), jnp.bfloat16),
            jax.ShapeDtypeStruct((8, PAIRS_B * WIDE), jnp.bfloat16),
        ],
        name="pack",
    )(query_weight, key_weight, value_weight)


def order_kernel(offsets, me_ref, *refs):
    pieces, out_ref = refs[:-1], refs[-1]
    count = len(pieces)
    for offset, piece in zip(offsets, pieces):
        out_ref[lax.rem(me_ref[0] + offset % count, count)] = piece[...]


def in_order(me, offsets, pieces):
    rows, columns = pieces[0].shape
    count = len(pieces)
    return pl.pallas_call(
        functools.partial(order_kernel, offsets),
        in_specs=[SMEM] + [VMEM] * count,
        out_specs=VMEM,
        out_shape=jax.ShapeDtypeStruct((count, rows, columns), jnp.bfloat16),
        name="in_order",
    )(me.reshape(1), *pieces).reshape(count * rows, columns)


def one_hot(source, first):
    at = lax.broadcasted_iota(jnp.int32, (128, source.shape[1]), 0) + first
    return jnp.where(at == source, 1.0, 0.0).astype(jnp.bfloat16)


def picked(rows, tiles, source):
    left = jnp.concatenate([rows(tile) for tile in tiles], axis=1)
    right = jnp.concatenate([one_hot(source, tile * 128) for tile in tiles], axis=0)
    return dot_f32(left, right).astype(jnp.bfloat16)


def late_source(c, tile, strip):
    z, core, xh, xl, r = 2 * tile + ((c >> 6) & 1), (c >> 5) & 1, (c >> 4) & 1, (c >> 3) & 1, c & 7
    return ((xh * 2 + core) * 16 + z * 2 + xl) * strip + r


def early_source(c, tile, strip):
    core, z, r = (c >> 6) & 1, (c >> 3) & 7, c & 7
    return ((tile // 2 * 2 + core) * 16 + z * 2 + tile % 2) * strip + r


def order_query_kernel(x_ref, late_ref, early_ref):
    column = lax.broadcasted_iota(jnp.int32, (1, 384), 1)
    c, j = column & 127, column >> 7
    rows = lambda tile: x_ref[:, tile * 128 : (tile + 1) * 128]
    for tile in range(4):
        low, high = 96 * tile // 128, (96 * tile + 95) // 128
        near = [3 * block + part for block in range(4) for part in range(low, high + 1)]
        late = picked(rows, near, late_source(c, tile, 24) + 8 * j)
        near = [3 * (tile // 2 * 2 + core) + part for core in range(2) for part in range(3)]
        early = picked(rows, near, early_source(c, tile, 24) + 8 * j)
        for strip in range(3):
            late_ref[strip, :, tile * 128 : (tile + 1) * 128] = late[:, strip * 128 : (strip + 1) * 128]
            early_ref[strip, :, tile * 128 : (tile + 1) * 128] = early[:, strip * 128 : (strip + 1) * 128]


def order_query(x):
    shape = jax.ShapeDtypeStruct((3, TOK, 512), jnp.bfloat16)
    return pl.pallas_call(
        order_query_kernel,
        in_specs=[VMEM],
        out_specs=[VMEM] * 2,
        out_shape=[shape, shape],
        compiler_params=pltpu.CompilerParams(vmem_limit_bytes=24 * MIB),
        cost_estimate=pl.CostEstimate(flops=2_500_000_000, bytes_accessed=6_000_000, transcendentals=0),
        name="order_query",
    )(x)


def order_latent_kernel(me_ref, own_ref, own_rope_ref, *refs):
    pieces, (late_ref, early_ref, rope_ref, prev_ref) = refs[:4], refs[4:]
    for offset, piece in zip((0, -1, 1, 2), pieces):
        slot = lax.rem(me_ref[0] + offset % 4, 4)
        prev_ref[pl.ds(pl.multiple_of(slot * 128, 128), 128), :] = piece[...]
    rope_ref[:TOK] = own_rope_ref[...]
    rope_ref[TOK:] = prev_ref[:, 512:]
    c = lax.broadcasted_iota(jnp.int32, (1, 128), 1)
    for part, ref in ((0, own_ref), (1, prev_ref)):
        rows = lambda tile: ref[:, tile * 128 : (tile + 1) * 128]
        for tile in range(4):
            at = slice(tile * 128, (tile + 1) * 128)
            late_ref[part * TOK : (part + 1) * TOK, at] = picked(rows, range(4), late_source(c, tile, 8))
            near = [tile // 2 * 2, tile // 2 * 2 + 1]
            early_ref[part * TOK : (part + 1) * TOK, at] = picked(rows, near, early_source(c, tile, 8))


def order_latent(me, own, own_rope, pieces):
    shape = jax.ShapeDtypeStruct((2 * TOK, 512), jnp.bfloat16)
    return pl.pallas_call(
        order_latent_kernel,
        in_specs=[SMEM] + [VMEM] * 6,
        out_specs=[VMEM] * 3,
        out_shape=[shape, shape, jax.ShapeDtypeStruct((2 * TOK, QK_ROPE), jnp.bfloat16)],
        scratch_shapes=[pltpu.VMEM((TOK, 512 + QK_ROPE), jnp.bfloat16)],
        compiler_params=pltpu.CompilerParams(vmem_limit_bytes=24 * MIB),
        cost_estimate=pl.CostEstimate(flops=1_000_000_000, bytes_accessed=4_000_000, transcendentals=0),
        name="order_latent",
    )(me.reshape(1), own, own_rope, *pieces)


def moved(block, axes, distance):
    count = lax.axis_size(axes)
    return lax.ppermute(block, axes, [(i, (i + distance) % count) for i in range(count)])


def local(query_latent, shared_latent, rope_keys, block_order, query_weight, key_weight, value_weight):
    heads = key_weight.shape[1] // QK_NOPE
    me_x = lax.axis_index(X).astype(jnp.int32)
    me_z = lax.axis_index("z").astype(jnp.int32)
    me_core = lax.axis_index("core").astype(jnp.int32)
    cycle = lax.axis_size(("z", "xl"))
    position = lax.axis_index(("z", "xl"))
    order_row = block_order[lax.axis_index(("xh", "core"))]
    seen = (order_row[(position - 1 + cycle) % cycle] < order_row[position]).astype(jnp.int32)
    place = jnp.stack([seen, me_x, me_core])

    packed_a, packed_b = pack(query_weight, key_weight, value_weight)

    barrier = lax.optimization_barrier
    me_t = lax.axis_index("tensor").astype(jnp.int32)
    quarter = TOK // lax.axis_size("tensor")
    latent, rope_own = shared_latent[0], rope_keys[0]

    along_x = [packed_a, moved(packed_a, X, 1), moved(packed_a, X, -1), moved(packed_a, X, 2)]
    shard_a = in_order(me_x, (0, -1, 1, 2), along_x)
    mine = jnp.concatenate(
        [lax.dynamic_slice_in_dim(a, me_t * quarter, quarter, 0) for a in (latent, rope_own)], axis=1
    )
    shard_a, mine, packed_b = barrier((shard_a, mine, packed_b))
    gathered_a = lax.all_gather(shard_a, ("z", "core"), axis=0, tiled=True)

    up, down = moved(packed_b, "z", 1), moved(packed_b, "z", -1)
    up2, down2 = moved(packed_b, "z", 2), moved(packed_b, "z", -2)
    up3, down3, up4 = moved(up, "z", 2), moved(down, "z", -2), moved(up2, "z", 2)
    own = in_order(me_z, (0, -1, 1, -2, 2, -3, 3, -4), [packed_b, up, down, up2, down2, up3, down3, up4])
    theirs = moved(mine, ("z", "xl"), 1)
    own, theirs = barrier((own, theirs))

    before, after = moved(own, X, 1), moved(own, X, -1)
    prev = [theirs, moved(theirs, "tensor", 1), moved(theirs, "tensor", -1), moved(theirs, "tensor", 2)]
    x_a, x_b = order_query(query_latent[0])
    before, after, x_a, x_b = barrier((before, after, x_a, x_b))
    far_low, far_high = moved(before[:32], X, 1), moved(after[32:], X, -1)
    lat_a, lat_b, rope = order_latent(me_t, latent, rope_own, prev)
    far_low, far_high, lat_a, lat_b, rope = barrier((far_low, far_high, lat_a, lat_b, rope))
    mine = [own, before, after, far_low, far_high]
    pieces = mine + [moved(piece, "core", 1) for piece in mine]

    done = attend(early_kernel, "early", PAIRS_A, PAIRS_B, 10, place, x_b, lat_b, rope, pieces)
    attended, peaks = attend(late_kernel, "late", 0, PAIRS_A, 1, place, x_a, lat_a, rope, [gathered_a], done)

    peaks = peaks[:, :PAIR, 0].reshape(1, heads)
    everyone = lax.axis_size(GROUP)
    shared = lax.all_to_all(jnp.broadcast_to(peaks[None], (everyone, 1, heads)), GROUP, 0, 0)
    logit_max = jnp.max(shared, axis=(0, 1))
    clip = TAU / jnp.maximum(logit_max, TAU)
    root = jnp.sqrt(clip)
    factors = jnp.concatenate(
        [jnp.broadcast_to(root[:, None], (heads, QK_NOPE)), jnp.broadcast_to(clip[:, None], (heads, QK_ROPE))], axis=1
    ).reshape(1, heads * HEAD)
    clipped_q = (query_weight.astype(jnp.float32) * factors).astype(jnp.bfloat16)
    clipped_k = (key_weight.astype(jnp.float32) * jnp.repeat(root, QK_NOPE)[None]).astype(jnp.bfloat16)
    return (attended[None], logit_max, clipped_q, clipped_k)


def solution(mesh):
    fine = Mesh(mesh.devices.reshape(2, 2, 8, 2, 4), ("xh", "core", "z", "xl", "tensor"))
    dp, ctx = ("xh", "core"), ("z", "xl")
    return jax.shard_map(
        local,
        mesh=fine,
        in_specs=(
            P(dp, ctx, None),
            P(dp, ctx, None),
            P(dp, ctx, None),
            P(),
            P(GROUP, "tensor"),
            P(GROUP, "tensor"),
            P(GROUP, "tensor"),
        ),
        out_specs=(
            P(dp, ctx, "tensor"),
            P("tensor"),
            P(GROUP, "tensor"),
            P(GROUP, "tensor"),
        ),
        check_vma=False,
    )
```

```python
import functools
import math

import jax
import jax.numpy as jnp
from jax import lax
from jax.experimental import pallas as pl
from jax.experimental.pallas import tpu as pltpu
from jax.sharding import Mesh
from jax.sharding import PartitionSpec as P

QK_NOPE = 128
QK_ROPE = 64
V_DIM = 128
TAU = 100
HEAD = QK_NOPE + QK_ROPE
SCALE = 1.0 / math.sqrt(HEAD)
SCALE2 = SCALE * math.log2(math.e)
FAR = 1e30

GROUP = ("xh", "core", "z", "xl")
X = ("xh", "xl")
TOK = 512
HALF = TOK // 2
PAIR = 2
Q_WIDE = PAIR * HEAD
K_WIDE = PAIR * QK_NOPE
WIDE = 3 * Q_WIDE + 2 * K_WIDE
PAIRS = 8
PAIRS_A = 5
PAIRS_B = PAIRS - PAIRS_A
MIB = 1024 * 1024
VMEM = pl.BlockSpec(memory_space=pltpu.VMEM)
SMEM = pl.BlockSpec(memory_space=pltpu.SMEM)
ANY = pl.BlockSpec(memory_space=pl.ANY)
HBM = pl.BlockSpec(memory_space=pltpu.HBM)


def whole(shape):
    return pl.BlockSpec(shape, lambda p: (0,) * len(shape))


EARLY_MIB = 20
LATE_MIB = 48


def dot_f32(a, b):
    return jnp.dot(a, b, preferred_element_type=jnp.float32)


def dot_t(a, b):
    return lax.dot_general(a, b, (((1,), (1,)), ((), ())), preferred_element_type=jnp.float32)


def attend_pair(seen, x_ref, lat_ref, rope_ref, weight, out_ref, peak_ref):
    query = functools.reduce(jnp.add, [dot_f32(x_ref[j], weight(j * Q_WIDE, Q_WIDE)) for j in range(3)])
    query = query.astype(jnp.bfloat16)
    keys = dot_f32(lat_ref[...], weight(3 * Q_WIDE, K_WIDE)).astype(jnp.bfloat16)
    values = dot_f32(lat_ref[...], weight(3 * Q_WIDE + K_WIDE, K_WIDE)).astype(jnp.bfloat16)
    rope = rope_ref[...]
    row = lax.broadcasted_iota(jnp.int32, (HALF, HALF), 0)
    col = lax.broadcasted_iota(jnp.int32, (HALF, HALF), 1)
    diagonal = col <= row
    ones = (lax.broadcasted_iota(jnp.int32, (2 * TOK, V_DIM), 1) == 0).astype(jnp.bfloat16)

    def logits_of(head, part):
        q_part = query[part * HALF : (part + 1) * HALF, head * HEAD : (head + 1) * HEAD]
        key_head = jnp.concatenate([keys[:, head * QK_NOPE : (head + 1) * QK_NOPE], rope], axis=1)
        spans = [(0, HALF, "all")] if part == 1 else []
        spans += [(part * HALF, HALF, "diag"), (TOK, TOK, "prev")]
        logits = []
        for start, size, kind in spans:
            s = dot_t(q_part, key_head[start : start + size])
            logits.append(jnp.where(diagonal, s, -jnp.inf) if kind == "diag" else s)
        return spans, logits

    def finish(head, part, spans, logits):
        value_head = jnp.concatenate([values[:, head * V_DIM : (head + 1) * V_DIM], ones], axis=1)
        peak = functools.reduce(jnp.maximum, [jnp.max(s, axis=1, keepdims=True) for s in logits[:-1]])
        prev_peak = jnp.max(logits[-1], axis=1, keepdims=True)
        peak = jnp.where(seen, jnp.maximum(peak, prev_peak), peak)
        shift = peak * SCALE2
        shift_prev = jnp.where(seen, shift, FAR)
        result = None
        for s, (start, size, kind) in zip(logits, spans):
            expo = jnp.exp2(s * SCALE2 - (shift_prev if kind == "prev" else shift))
            term = dot_f32(expo.astype(jnp.bfloat16), value_head[start : start + size])
            result = term if result is None else result + term
        result = result[:, :V_DIM] * (1.0 / result[:, V_DIM : V_DIM + 1])
        out_ref[part * HALF : (part + 1) * HALF, head * V_DIM : (head + 1) * V_DIM] = result.astype(jnp.bfloat16)
        return jnp.max(peak)

    order = [(head, part) for head in range(PAIR) for part in range(2)]
    peaks = []
    current = logits_of(*order[0])
    for i, (head, part) in enumerate(order):
        following = logits_of(*order[i + 1]) if i + 1 < len(order) else None
        peaks.append(finish(head, part, *current))
        current = following
    for head in range(PAIR):
        top = jnp.maximum(peaks[2 * head], peaks[2 * head + 1]) * SCALE
        peak_ref[0, head : head + 1, :] = jnp.broadcast_to(top, (1, 128))


def in_slots(pairs, copies, w_ref, sems):
    pair = pl.program_id(0)
    slot = lax.rem(pair, 2)

    @pl.when(pair == 0)
    def _():
        for copy in copies(0, 0):
            copy.start()

    @pl.when(pair + 1 < pairs)
    def _():
        for copy in copies(pair + 1, 1 - slot):
            copy.start()

    for copy in copies(pair, slot):
        copy.wait()
    return lambda start, width: w_ref[slot, :, start : start + width]


def late_kernel(place_ref, x_ref, lat_ref, rope_ref, all_ref, *rest):
    out_ref, peak_ref, w_ref, sems = rest[-4:]

    def copies(pair, slot):
        columns = pl.ds(pl.multiple_of(pair * WIDE, 128), WIDE)
        return [pltpu.make_async_copy(all_ref.at[:, columns], w_ref.at[slot], sems.at[slot, 0])]

    weight = in_slots(PAIRS_A, copies, w_ref, sems)
    attend_pair(place_ref[0] > 0, x_ref, lat_ref, rope_ref, weight, out_ref, peak_ref)


def early_kernel(place_ref, x_ref, lat_ref, rope_ref, *rest):
    pieces, (out_ref, peak_ref, w_ref, sems) = rest[:10], rest[-4:]
    me, core = place_ref[1], place_ref[2]

    def copies(pair, slot):
        columns = pl.ds(pl.multiple_of(pair * WIDE, 128), WIDE)
        made = []
        for side in range(2):
            owner = core if side == 0 else 1 - core
            for piece, step, first in zip(pieces[5 * side : 5 * side + 5], (0, 3, 1, 2, 2), (0, 0, 0, 0, 32)):
                block = lax.rem(me + step, 4) * 2 + owner
                rows = pl.ds(pl.multiple_of(block * 64 + first, 32), piece.shape[0])
                made.append(
                    pltpu.make_async_copy(piece.at[:, columns], w_ref.at[slot, rows, :], sems.at[slot, len(made)])
                )
        return made

    weight = in_slots(PAIRS_B, copies, w_ref, sems)
    attend_pair(place_ref[0] > 0, x_ref, lat_ref, rope_ref, weight, out_ref, peak_ref)


def attend(kernel, name, first, pairs, copies, place, x, latents, rope, weights, before=()):
    return pl.pallas_call(
        kernel,
        grid=(pairs,),
        in_specs=[SMEM] + [whole(a.shape) for a in (x, latents, rope)] + [HBM if len(weights) == 1 else ANY] * len(weights) + [ANY] * len(before),
        out_specs=[
            pl.BlockSpec((TOK, PAIR * V_DIM), lambda p: (0, first + p)),
            pl.BlockSpec((1, 8, 128), lambda p: (first + p, 0, 0)),
        ],
        out_shape=[
            jax.ShapeDtypeStruct((TOK, PAIRS * PAIR * V_DIM), jnp.bfloat16),
            jax.ShapeDtypeStruct((PAIRS, 8, 128), jnp.float32),
        ],
        input_output_aliases={4 + len(weights) + i: i for i in range(len(before))},
        scratch_shapes=[
            pltpu.VMEM((2, TOK, WIDE), jnp.bfloat16),
            pltpu.SemaphoreType.DMA((2, copies)),
        ],
        compiler_params=pltpu.CompilerParams(vmem_limit_bytes=(LATE_MIB if before else EARLY_MIB) * MIB),
        cost_estimate=pl.CostEstimate(
            flops=1_800_000_000 * pairs, bytes_accessed=2_000_000 * pairs, transcendentals=1_000_000 * pairs
        ),
        name=name,
    )(place, x, latents, rope, *weights, *before)


def pack_kernel(q_ref, k_ref, v_ref, a_ref, b_ref):
    for pair in range(PAIRS):
        ref, at = (a_ref, pair) if pair < PAIRS_A else (b_ref, pair - PAIRS_A)
        at = at * WIDE
        for j in range(3):
            ref[:, at + j * Q_WIDE : at + (j + 1) * Q_WIDE] = q_ref[8 * j : 8 * j + 8, pair * Q_WIDE : (pair + 1) * Q_WIDE]
        at += 3 * Q_WIDE
        ref[:, at : at + K_WIDE] = k_ref[:, pair * K_WIDE : (pair + 1) * K_WIDE]
        ref[:, at + K_WIDE : at + 2 * K_WIDE] = v_ref[:, pair * K_WIDE : (pair + 1) * K_WIDE]


def pack(query_weight, key_weight, value_weight):
    return pl.pallas_call(
        pack_kernel,
        in_specs=[VMEM] * 3,
        out_specs=[VMEM] * 2,
        out_shape=[
            jax.ShapeDtypeStruct((8, PAIRS_A * WIDE), jnp.bfloat16),
            jax.ShapeDtypeStruct((8, PAIRS_B * WIDE), jnp.bfloat16),
        ],
        compiler_params=pltpu.CompilerParams(vmem_limit_bytes=4 * MIB),
        name="pack",
    )(query_weight, key_weight, value_weight)


def order_kernel(offsets, me_ref, *refs):
    pieces, out_ref = refs[:-1], refs[-1]
    count = len(pieces)
    for offset, piece in zip(offsets, pieces):
        out_ref[lax.rem(me_ref[0] + offset % count, count)] = piece[...]


def in_order(me, offsets, pieces):
    rows, columns = pieces[0].shape
    count = len(pieces)
    return pl.pallas_call(
        functools.partial(order_kernel, offsets),
        in_specs=[SMEM] + [VMEM] * count,
        out_specs=VMEM,
        out_shape=jax.ShapeDtypeStruct((count, rows, columns), jnp.bfloat16),
        compiler_params=pltpu.CompilerParams(vmem_limit_bytes=4 * MIB),
        name="in_order",
    )(me.reshape(1), *pieces).reshape(count * rows, columns)


def halves_kernel(before_ref, after_ref, low_ref, high_ref):
    low_ref[...] = before_ref[:32]
    high_ref[...] = after_ref[32:]


def halves(before, after):
    shape = jax.ShapeDtypeStruct((32, before.shape[1]), before.dtype)
    return pl.pallas_call(
        halves_kernel,
        in_specs=[VMEM] * 2,
        out_specs=[VMEM] * 2,
        out_shape=[shape, shape],
        compiler_params=pltpu.CompilerParams(vmem_limit_bytes=4 * MIB),
        name="halves",
    )(before, after)


def one_hot(source, first):
    at = lax.broadcasted_iota(jnp.int32, (128, source.shape[1]), 0) + first
    return jnp.where(at == source, 1.0, 0.0).astype(jnp.bfloat16)


def picked(rows, tiles, source):
    left = jnp.concatenate([rows(tile) for tile in tiles], axis=1)
    right = jnp.concatenate([one_hot(source, tile * 128) for tile in tiles], axis=0)
    return dot_f32(left, right).astype(jnp.bfloat16)


def late_source(c, tile, strip):
    z, core, xh, xl, r = 2 * tile + ((c >> 6) & 1), (c >> 5) & 1, (c >> 4) & 1, (c >> 3) & 1, c & 7
    return ((xh * 2 + core) * 16 + z * 2 + xl) * strip + r


def early_source(c, tile, strip):
    core, z, r = (c >> 6) & 1, (c >> 3) & 7, c & 7
    return ((tile // 2 * 2 + core) * 16 + z * 2 + tile % 2) * strip + r


def order_query_kernel(x_ref, late_ref, early_ref):
    column = lax.broadcasted_iota(jnp.int32, (1, 384), 1)
    c, j = column & 127, column >> 7
    rows = lambda tile: x_ref[:, tile * 128 : (tile + 1) * 128]
    for tile in range(4):
        low, high = 96 * tile // 128, (96 * tile + 95) // 128
        near = [3 * block + part for block in range(4) for part in range(low, high + 1)]
        late = picked(rows, near, late_source(c, tile, 24) + 8 * j)
        near = [3 * (tile // 2 * 2 + core) + part for core in range(2) for part in range(3)]
        early = picked(rows, near, early_source(c, tile, 24) + 8 * j)
        for strip in range(3):
            late_ref[strip, :, tile * 128 : (tile + 1) * 128] = late[:, strip * 128 : (strip + 1) * 128]
            early_ref[strip, :, tile * 128 : (tile + 1) * 128] = early[:, strip * 128 : (strip + 1) * 128]


def order_query(x):
    shape = jax.ShapeDtypeStruct((3, TOK, 512), jnp.bfloat16)
    return pl.pallas_call(
        order_query_kernel,
        grid=(1,),
        in_specs=[whole(x.shape)],
        out_specs=[whole(shape.shape)] * 2,
        out_shape=[shape, shape],
        compiler_params=pltpu.CompilerParams(vmem_limit_bytes=16 * MIB),
        cost_estimate=pl.CostEstimate(flops=2_500_000_000, bytes_accessed=6_000_000, transcendentals=0),
        name="order_query",
    )(x)


def order_latent_kernel(me_ref, own_ref, own_rope_ref, *refs):
    pieces, (late_ref, early_ref, rope_ref, prev_ref) = refs[:4], refs[4:]
    for offset, piece in zip((0, -1, 1, 2), pieces):
        slot = lax.rem(me_ref[0] + offset % 4, 4)
        prev_ref[pl.ds(pl.multiple_of(slot * 128, 128), 128), :] = piece[...]
    rope_ref[:TOK] = own_rope_ref[...]
    rope_ref[TOK:] = prev_ref[:, 512:]
    c = lax.broadcasted_iota(jnp.int32, (1, 128), 1)
    for part, ref in ((0, own_ref), (1, prev_ref)):
        rows = lambda tile: ref[:, tile * 128 : (tile + 1) * 128]
        for tile in range(4):
            at = slice(tile * 128, (tile + 1) * 128)
            late_ref[part * TOK : (part + 1) * TOK, at] = picked(rows, range(4), late_source(c, tile, 8))
            near = [tile // 2 * 2, tile // 2 * 2 + 1]
            early_ref[part * TOK : (part + 1) * TOK, at] = picked(rows, near, early_source(c, tile, 8))


def order_latent(me, own, own_rope, pieces):
    operands = (own, own_rope, *pieces)
    shapes = [jax.ShapeDtypeStruct((2 * TOK, width), jnp.bfloat16) for width in (512, 512, QK_ROPE)]
    return pl.pallas_call(
        order_latent_kernel,
        grid=(1,),
        in_specs=[SMEM] + [whole(a.shape) for a in operands],
        out_specs=[whole(a.shape) for a in shapes],
        out_shape=shapes,
        scratch_shapes=[pltpu.VMEM((TOK, 512 + QK_ROPE), jnp.bfloat16)],
        compiler_params=pltpu.CompilerParams(vmem_limit_bytes=16 * MIB),
        cost_estimate=pl.CostEstimate(flops=1_000_000_000, bytes_accessed=4_000_000, transcendentals=0),
        name="order_latent",
    )(me.reshape(1), *operands)


def moved(block, axes, distance):
    count = lax.axis_size(axes)
    return lax.ppermute(block, axes, [(i, (i + distance) % count) for i in range(count)])


def local(query_latent, shared_latent, rope_keys, block_order, query_weight, key_weight, value_weight):
    heads = key_weight.shape[1] // QK_NOPE
    me_x = lax.axis_index(X).astype(jnp.int32)
    me_z = lax.axis_index("z").astype(jnp.int32)
    me_core = lax.axis_index("core").astype(jnp.int32)
    cycle = lax.axis_size(("z", "xl"))
    position = lax.axis_index(("z", "xl"))
    order_row = block_order[lax.axis_index(("xh", "core"))]
    seen = (order_row[(position - 1 + cycle) % cycle] < order_row[position]).astype(jnp.int32)
    place = jnp.stack([seen, me_x, me_core])

    packed_a, packed_b = pack(query_weight, key_weight, value_weight)

    barrier = lax.optimization_barrier
    me_t = lax.axis_index("tensor").astype(jnp.int32)
    quarter = TOK // lax.axis_size("tensor")
    latent, rope_own = shared_latent[0], rope_keys[0]

    along_x = [packed_a, moved(packed_a, X, 1), moved(packed_a, X, -1), moved(packed_a, X, 2)]
    shard_a = in_order(me_x, (0, -1, 1, 2), along_x)
    mine = jnp.concatenate(
        [lax.dynamic_slice_in_dim(a, me_t * quarter, quarter, 0) for a in (latent, rope_own)], axis=1
    )
    shard_a, mine, packed_b, place, rope_own = barrier((shard_a, mine, packed_b, place, rope_own))
    gathered_a = lax.all_gather(shard_a, ("z", "core"), axis=0, tiled=True)

    up, down = moved(packed_b, "z", 1), moved(packed_b, "z", -1)
    up2, down2 = moved(packed_b, "z", 2), moved(packed_b, "z", -2)
    up3, down3, up4 = moved(up, "z", 2), moved(down, "z", -2), moved(up2, "z", 2)
    own = in_order(me_z, (0, -1, 1, -2, 2, -3, 3, -4), [packed_b, up, down, up2, down2, up3, down3, up4])
    theirs = moved(mine, ("z", "xl"), 1)
    own, theirs = barrier((own, theirs))

    before, after = moved(own, X, 1), moved(own, X, -1)
    prev = [theirs, moved(theirs, "tensor", 1), moved(theirs, "tensor", -1), moved(theirs, "tensor", 2)]
    x_a, x_b = order_query(query_latent[0])
    before, after, x_a, x_b = barrier((before, after, x_a, x_b))
    low, high = halves(before, after)
    far_low, far_high = moved(low, X, 1), moved(high, X, -1)
    lat_a, lat_b, rope = order_latent(me_t, latent, rope_own, prev)
    far_low, far_high, lat_a, lat_b, rope = barrier((far_low, far_high, lat_a, lat_b, rope))
    mine = [own, before, after, far_low, far_high]
    pieces = mine + [moved(piece, "core", 1) for piece in mine]

    done = attend(early_kernel, "early", PAIRS_A, PAIRS_B, 10, place, x_b, lat_b, rope, pieces)
    attended, peaks = attend(late_kernel, "late", 0, PAIRS_A, 1, place, x_a, lat_a, rope, [gathered_a], done)

    peaks = peaks[:, :PAIR, 0].reshape(1, heads)
    everyone = lax.axis_size(GROUP)
    shared = lax.all_to_all(jnp.broadcast_to(peaks[None], (everyone, 1, heads)), GROUP, 0, 0)
    logit_max = jnp.max(shared, axis=(0, 1))
    clip = TAU / jnp.maximum(logit_max, TAU)
    root = jnp.sqrt(clip)
    factors = jnp.concatenate(
        [jnp.broadcast_to(root[:, None], (heads, QK_NOPE)), jnp.broadcast_to(clip[:, None], (heads, QK_ROPE))], axis=1
    ).reshape(1, heads * HEAD)
    clipped_q = (query_weight.astype(jnp.float32) * factors).astype(jnp.bfloat16)
    clipped_k = (key_weight.astype(jnp.float32) * jnp.repeat(root, QK_NOPE)[None]).astype(jnp.bfloat16)
    return (attended[None], logit_max, clipped_q, clipped_k)


def solution(mesh):
    fine = Mesh(mesh.devices.reshape(2, 2, 8, 2, 4), ("xh", "core", "z", "xl", "tensor"))
    dp, ctx = ("xh", "core"), ("z", "xl")
    return jax.shard_map(
        local,
        mesh=fine,
        in_specs=(
            P(dp, ctx, None),
            P(dp, ctx, None),
            P(dp, ctx, None),
            P(),
            P(GROUP, "tensor"),
            P(GROUP, "tensor"),
            P(GROUP, "tensor"),
        ),
        out_specs=(
            P(dp, ctx, "tensor"),
            P("tensor"),
            P(GROUP, "tensor"),
            P(GROUP, "tensor"),
        ),
        check_vma=False,
    )
```

```python
import functools
import math

import jax
import jax.numpy as jnp
from jax import lax
from jax.experimental import pallas as pl
from jax.experimental.pallas import tpu as pltpu
from jax.sharding import Mesh
from jax.sharding import PartitionSpec as P

QK_NOPE = 128
QK_ROPE = 64
V_DIM = 128
TAU = 100
HEAD = QK_NOPE + QK_ROPE
SCALE = 1.0 / math.sqrt(HEAD)
SCALE2 = SCALE * math.log2(math.e)
FAR = 1e30

GROUP = ("xh", "core", "z", "xl")
X = ("xh", "xl")
TOK = 512
HALF = TOK // 2
GROUPS_A = (4, 4, 2)
GROUPS_B = (4, 2)
HEADS_A = sum(GROUPS_A)
HEADS_B = sum(GROUPS_B)
WIDE = 3 * HEAD + QK_NOPE + V_DIM
MIB = 1024 * 1024
VMEM = pl.BlockSpec(memory_space=pltpu.VMEM)
SMEM = pl.BlockSpec(memory_space=pltpu.SMEM)
ANY = pl.BlockSpec(memory_space=pl.ANY)


def in_hbm(array):
    return pltpu.with_memory_space_constraint(array, pltpu.HBM)


def whole(shape):
    return pl.BlockSpec(shape, lambda p: (0,) * len(shape))


def dot_f32(a, b):
    return jnp.dot(a, b, preferred_element_type=jnp.float32)


def dot_t(a, b):
    return lax.dot_general(a, b, (((1,), (1,)), ((), ())), preferred_element_type=jnp.float32)


def attend_some(heads, seen, x_ref, lat_ref, rope_ref, weight, wait_query, out_ref, peak_ref):
    at = 3 * heads * HEAD
    keys = dot_f32(lat_ref[...], weight(at, heads * QK_NOPE)).astype(jnp.bfloat16)
    values = dot_f32(lat_ref[...], weight(at + heads * QK_NOPE, heads * V_DIM)).astype(jnp.bfloat16)
    wait_query()
    query = [dot_f32(x_ref[j], weight(j * heads * HEAD, heads * HEAD)) for j in range(3)]
    query = functools.reduce(jnp.add, query).astype(jnp.bfloat16)
    rope = rope_ref[...]
    row = lax.broadcasted_iota(jnp.int32, (HALF, HALF), 0)
    col = lax.broadcasted_iota(jnp.int32, (HALF, HALF), 1)
    diagonal = col <= row
    ones = (lax.broadcasted_iota(jnp.int32, (2 * TOK, V_DIM), 1) == 0).astype(jnp.bfloat16)

    def logits_of(head, part):
        q_part = query[part * HALF : (part + 1) * HALF, head * HEAD : (head + 1) * HEAD]
        key_head = jnp.concatenate([keys[:, head * QK_NOPE : (head + 1) * QK_NOPE], rope], axis=1)
        spans = [(0, HALF, "all")] if part == 1 else []
        spans += [(part * HALF, HALF, "diag"), (TOK, TOK, "prev")]
        logits = []
        for start, size, kind in spans:
            s = dot_t(q_part, key_head[start : start + size])
            logits.append(jnp.where(diagonal, s, -jnp.inf) if kind == "diag" else s)
        return spans, logits

    def finish(head, part, spans, logits):
        value_head = jnp.concatenate([values[:, head * V_DIM : (head + 1) * V_DIM], ones], axis=1)
        peak = functools.reduce(jnp.maximum, [jnp.max(s, axis=1, keepdims=True) for s in logits[:-1]])
        prev_peak = jnp.max(logits[-1], axis=1, keepdims=True)
        peak = jnp.where(seen, jnp.maximum(peak, prev_peak), peak)
        shift = peak * SCALE2
        shift_prev = jnp.where(seen, shift, FAR)
        result = None
        for s, (start, size, kind) in zip(logits, spans):
            expo = jnp.exp2(s * SCALE2 - (shift_prev if kind == "prev" else shift))
            term = dot_f32(expo.astype(jnp.bfloat16), value_head[start : start + size])
            result = term if result is None else result + term
        result = result[:, :V_DIM] * (1.0 / result[:, V_DIM : V_DIM + 1])
        out_ref[part * HALF : (part + 1) * HALF, head * V_DIM : (head + 1) * V_DIM] = result.astype(jnp.bfloat16)
        return jnp.max(peak)

    order = [(head, part) for head in range(heads) for part in range(2)]
    peaks = []
    current = logits_of(*order[0])
    for i, (head, part) in enumerate(order):
        following = logits_of(*order[i + 1]) if i + 1 < len(order) else None
        peaks.append(finish(head, part, *current))
        current = following
    for head in range(heads):
        top = jnp.maximum(peaks[2 * head], peaks[2 * head + 1]) * SCALE
        peak_ref[head : head + 1, :] = jnp.broadcast_to(top, (1, 128))


def from_gathered(place_ref, pieces):
    return [(pieces[0], pl.ds(0, TOK))]


def from_ring(place_ref, pieces):
    me, core = place_ref[1], place_ref[2]
    made = []
    for side in range(2):
        owner = core if side == 0 else 1 - core
        for piece, distance, first in zip(pieces[5 * side : 5 * side + 5], (0, 3, 1, 2, 2), (0, 0, 0, 0, 32)):
            block = lax.rem(me + distance, 4) * 2 + owner
            made.append((piece, pl.ds(pl.multiple_of(block * 64 + first, 32), piece.shape[0])))
    return made


def attend_kernel(rows_of, groups, first, count, place_ref, x_ref, lat_ref, rope_ref, *rest):
    pieces = rest[:count]
    out_hbm, peak_ref, w_ref, out_ref, sems, out_sems = rest[-6:]
    rows = rows_of(place_ref, pieces)
    starts = [sum(groups[:i]) for i in range(len(groups))]

    def copies(group, part):
        heads, start = groups[group], starts[group] * WIDE
        split = 3 * heads * HEAD
        columns = pl.ds(start + split, heads * WIDE - split) if part == 0 else pl.ds(start, split)
        return [
            pltpu.make_async_copy(piece.at[:, columns], w_ref.at[where, columns], sems.at[group, part, i])
            for i, (piece, where) in enumerate(rows)
        ]

    def start(group):
        for part in range(2):
            for copy in copies(group, part):
                copy.start()

    start(0)
    results = []
    for group, heads in enumerate(groups):

        def wait(part, group=group):
            for copy in copies(group, part):
                copy.wait()

        def wait_query(group=group, wait=wait):
            wait(1)
            if group + 1 < len(groups):
                start(group + 1)

        def weight(at, width, group=group):
            at = starts[group] * WIDE + at
            return w_ref[:, at : at + width]

        wait(0)
        here = pl.ds(starts[group] * V_DIM, heads * V_DIM)
        out = out_ref.at[:, here]
        peak = peak_ref.at[pl.ds(starts[group], heads), :]
        attend_some(heads, place_ref[0] > 0, x_ref, lat_ref, rope_ref, weight, wait_query, out, peak)
        there = pl.ds((first + starts[group]) * V_DIM, heads * V_DIM)
        results.append(pltpu.make_async_copy(out, out_hbm.at[:, there], out_sems.at[group]))
        results[-1].start()
    for result in results:
        result.wait()


def attend(rows_of, groups, first, name, place, x, latents, rope, pieces, before=()):
    heads, count = sum(groups), len(pieces)
    return pl.pallas_call(
        functools.partial(attend_kernel, rows_of, groups, first, count),
        grid=(1,),
        in_specs=[SMEM] + [whole(a.shape) for a in (x, latents, rope)] + [ANY] * (count + len(before)),
        out_specs=[ANY, whole((16, 128))],
        out_shape=[
            jax.ShapeDtypeStruct((TOK, (HEADS_A + HEADS_B) * V_DIM), jnp.bfloat16),
            jax.ShapeDtypeStruct((16, 128), jnp.float32),
        ],
        input_output_aliases={4 + count: 0} if before else {},
        scratch_shapes=[
            pltpu.VMEM((TOK, heads * WIDE), jnp.bfloat16),
            pltpu.VMEM((TOK, heads * V_DIM), jnp.bfloat16),
            pltpu.SemaphoreType.DMA((len(groups), 2, count)),
            pltpu.SemaphoreType.DMA((len(groups),)),
        ],
        compiler_params=pltpu.CompilerParams(vmem_limit_bytes=(40 if before else 24) * MIB),
        cost_estimate=pl.CostEstimate(
            flops=900_000_000 * heads, bytes_accessed=1_000_000 * heads, transcendentals=500_000 * heads
        ),
        name=name,
    )(place, x, latents, rope, *pieces, *before)


def pack_kernel(q_ref, k_ref, v_ref, a_ref, b_ref):
    head = 0
    for groups, ref in ((GROUPS_A, a_ref), (GROUPS_B, b_ref)):
        at = 0
        for heads in groups:
            for j in range(3):
                columns = slice(head * HEAD, (head + heads) * HEAD)
                ref[:, at : at + heads * HEAD] = q_ref[8 * j : 8 * j + 8, columns]
                at += heads * HEAD
            for source in (k_ref, v_ref):
                ref[:, at : at + heads * QK_NOPE] = source[:, head * QK_NOPE : (head + heads) * QK_NOPE]
                at += heads * QK_NOPE
            head += heads


def pack(*weights):
    shapes = [jax.ShapeDtypeStruct((8, heads * WIDE), jnp.bfloat16) for heads in (HEADS_A, HEADS_B)]
    return pl.pallas_call(
        pack_kernel,
        grid=(1,),
        in_specs=[whole(a.shape) for a in weights],
        out_specs=[whole(a.shape) for a in shapes],
        out_shape=shapes,
        compiler_params=pltpu.CompilerParams(vmem_limit_bytes=8 * MIB),
        name="pack",
    )(*[in_hbm(a) for a in weights])


def order_kernel(offsets, me_ref, *refs):
    pieces, out_ref = refs[:-1], refs[-1]
    count = len(pieces)
    for offset, piece in zip(offsets, pieces):
        out_ref[lax.rem(me_ref[0] + offset % count, count)] = piece[...]


def in_order(me, offsets, pieces):
    rows, columns = pieces[0].shape
    count = len(pieces)
    return pl.pallas_call(
        functools.partial(order_kernel, offsets),
        in_specs=[SMEM] + [VMEM] * count,
        out_specs=VMEM,
        out_shape=jax.ShapeDtypeStruct((count, rows, columns), jnp.bfloat16),
        compiler_params=pltpu.CompilerParams(vmem_limit_bytes=4 * MIB),
        name="in_order",
    )(me.reshape(1), *pieces).reshape(count * rows, columns)


def halves_kernel(before_ref, after_ref, low_ref, high_ref):
    low_ref[...] = before_ref[:32]
    high_ref[...] = after_ref[32:]


def halves(before, after):
    shape = jax.ShapeDtypeStruct((32, before.shape[1]), before.dtype)
    return pl.pallas_call(
        halves_kernel,
        in_specs=[VMEM] * 2,
        out_specs=[VMEM] * 2,
        out_shape=[shape, shape],
        compiler_params=pltpu.CompilerParams(vmem_limit_bytes=4 * MIB),
        name="halves",
    )(before, after)


def one_hot(source, first):
    at = lax.broadcasted_iota(jnp.int32, (128, source.shape[1]), 0) + first
    return jnp.where(at == source, 1.0, 0.0).astype(jnp.bfloat16)


def picked(rows, tiles, source):
    left = jnp.concatenate([rows(tile) for tile in tiles], axis=1)
    right = jnp.concatenate([one_hot(source, tile * 128) for tile in tiles], axis=0)
    return dot_f32(left, right).astype(jnp.bfloat16)


def late_source(c, tile, strip):
    z, core, xh, xl, r = 2 * tile + ((c >> 6) & 1), (c >> 5) & 1, (c >> 4) & 1, (c >> 3) & 1, c & 7
    return ((xh * 2 + core) * 16 + z * 2 + xl) * strip + r


def early_source(c, tile, strip):
    core, z, r = (c >> 6) & 1, (c >> 3) & 7, c & 7
    return ((tile // 2 * 2 + core) * 16 + z * 2 + tile % 2) * strip + r


def order_query_kernel(x_ref, late_ref, early_ref):
    column = lax.broadcasted_iota(jnp.int32, (1, 384), 1)
    c, j = column & 127, column >> 7
    rows = lambda tile: x_ref[:, tile * 128 : (tile + 1) * 128]
    for tile in range(4):
        low, high = 96 * tile // 128, (96 * tile + 95) // 128
        near = [3 * block + part for block in range(4) for part in range(low, high + 1)]
        late = picked(rows, near, late_source(c, tile, 24) + 8 * j)
        near = [3 * (tile // 2 * 2 + core) + part for core in range(2) for part in range(3)]
        early = picked(rows, near, early_source(c, tile, 24) + 8 * j)
        for strip in range(3):
            late_ref[strip, :, tile * 128 : (tile + 1) * 128] = late[:, strip * 128 : (strip + 1) * 128]
            early_ref[strip, :, tile * 128 : (tile + 1) * 128] = early[:, strip * 128 : (strip + 1) * 128]


def order_query(x):
    shape = jax.ShapeDtypeStruct((3, TOK, 512), jnp.bfloat16)
    return pl.pallas_call(
        order_query_kernel,
        grid=(1,),
        in_specs=[whole(x.shape)],
        out_specs=[whole(shape.shape)] * 2,
        out_shape=[shape, shape],
        compiler_params=pltpu.CompilerParams(vmem_limit_bytes=16 * MIB),
        cost_estimate=pl.CostEstimate(flops=2_500_000_000, bytes_accessed=6_000_000, transcendentals=0),
        name="order_query",
    )(x)


def order_latent_kernel(me_ref, own_ref, own_rope_ref, *refs):
    pieces, (late_ref, early_ref, rope_ref, prev_ref) = refs[:4], refs[4:]
    for offset, piece in zip((0, -1, 1, 2), pieces):
        slot = lax.rem(me_ref[0] + offset % 4, 4)
        prev_ref[pl.ds(pl.multiple_of(slot * 128, 128), 128), :] = piece[...]
    rope_ref[:TOK] = own_rope_ref[...]
    rope_ref[TOK:] = prev_ref[:, 512:]
    c = lax.broadcasted_iota(jnp.int32, (1, 128), 1)
    for part, ref in ((0, own_ref), (1, prev_ref)):
        rows = lambda tile: ref[:, tile * 128 : (tile + 1) * 128]
        for tile in range(4):
            at = slice(tile * 128, (tile + 1) * 128)
            late_ref[part * TOK : (part + 1) * TOK, at] = picked(rows, range(4), late_source(c, tile, 8))
            near = [tile // 2 * 2, tile // 2 * 2 + 1]
            early_ref[part * TOK : (part + 1) * TOK, at] = picked(rows, near, early_source(c, tile, 8))


def order_latent(me, own, own_rope, pieces):
    operands = (own, own_rope, *pieces)
    shapes = [jax.ShapeDtypeStruct((2 * TOK, width), jnp.bfloat16) for width in (512, 512, QK_ROPE)]
    return pl.pallas_call(
        order_latent_kernel,
        grid=(1,),
        in_specs=[SMEM] + [whole(a.shape) for a in operands],
        out_specs=[whole(a.shape) for a in shapes],
        out_shape=shapes,
        scratch_shapes=[pltpu.VMEM((TOK, 512 + QK_ROPE), jnp.bfloat16)],
        compiler_params=pltpu.CompilerParams(vmem_limit_bytes=16 * MIB),
        cost_estimate=pl.CostEstimate(flops=1_000_000_000, bytes_accessed=4_000_000, transcendentals=0),
        name="order_latent",
    )(me.reshape(1), *operands)


def moved(block, axes, distance):
    count = lax.axis_size(axes)
    return lax.ppermute(block, axes, [(i, (i + distance) % count) for i in range(count)])


def local(query_latent, shared_latent, rope_keys, block_order, query_weight, key_weight, value_weight):
    heads = key_weight.shape[1] // QK_NOPE
    me_x = lax.axis_index(X).astype(jnp.int32)
    me_z = lax.axis_index("z").astype(jnp.int32)
    me_core = lax.axis_index("core").astype(jnp.int32)
    cycle = lax.axis_size(("z", "xl"))
    packed_a, packed_b = pack(query_weight, key_weight, value_weight)

    barrier = lax.optimization_barrier
    me_t = lax.axis_index("tensor").astype(jnp.int32)
    quarter = TOK // lax.axis_size("tensor")

    along_x = [packed_a, moved(packed_a, X, 1), moved(packed_a, X, -1), moved(packed_a, X, 2)]
    shard_a = in_order(me_x, (0, -1, 1, 2), along_x)
    shard_a, latent, rope_own, block_order = barrier((shard_a, shared_latent[0], rope_keys[0], block_order))
    gathered_a = lax.all_gather(shard_a, ("z", "core"), axis=0, tiled=True)

    position = lax.axis_index(("z", "xl"))
    order_row = block_order[lax.axis_index(("xh", "core"))]
    seen = (order_row[(position - 1 + cycle) % cycle] < order_row[position]).astype(jnp.int32)
    place = jnp.stack([seen, me_x, me_core])
    mine = jnp.concatenate(
        [lax.dynamic_slice_in_dim(a, me_t * quarter, quarter, 0) for a in (latent, rope_own)], axis=1
    )
    up, down = moved(packed_b, "z", 1), moved(packed_b, "z", -1)
    up2, down2 = moved(packed_b, "z", 2), moved(packed_b, "z", -2)
    up3, down3, up4 = moved(up, "z", 2), moved(down, "z", -2), moved(up2, "z", 2)
    own = in_order(me_z, (0, -1, 1, -2, 2, -3, 3, -4), [packed_b, up, down, up2, down2, up3, down3, up4])
    theirs = moved(mine, ("z", "xl"), 1)
    own, theirs, place, rope_own = barrier((own, theirs, place, rope_own))

    before, after = moved(own, X, 1), moved(own, X, -1)
    prev = [theirs, moved(theirs, "tensor", 1), moved(theirs, "tensor", -1), moved(theirs, "tensor", 2)]
    x_a, x_b = order_query(query_latent[0])
    before, after, x_a, x_b = barrier((before, after, x_a, x_b))
    low, high = halves(before, after)
    far_low, far_high = moved(low, X, 1), moved(high, X, -1)
    lat_a, lat_b, rope = order_latent(me_t, latent, rope_own, prev)
    far_low, far_high, lat_a, lat_b, rope = barrier((far_low, far_high, lat_a, lat_b, rope))
    mine = [own, before, after, far_low, far_high]
    pieces = mine + [moved(piece, "core", 1) for piece in mine]

    out, peaks_b = attend(from_ring, GROUPS_B, HEADS_A, "ringed", place, x_b, lat_b, rope, pieces)
    gathered_a = [in_hbm(gathered_a)]
    attended, peaks_a = attend(from_gathered, GROUPS_A, 0, "gathered", place, x_a, lat_a, rope, gathered_a, [out])

    peaks = jnp.concatenate([peaks_a[:HEADS_A, 0], peaks_b[:HEADS_B, 0]]).reshape(1, heads)
    everyone = lax.axis_size(GROUP)
    shared = lax.all_to_all(jnp.broadcast_to(peaks[None], (everyone, 1, heads)), GROUP, 0, 0)
    logit_max = jnp.max(shared, axis=(0, 1))
    clip = TAU / jnp.maximum(logit_max, TAU)
    root = jnp.sqrt(clip)
    factors = jnp.concatenate(
        [jnp.broadcast_to(root[:, None], (heads, QK_NOPE)), jnp.broadcast_to(clip[:, None], (heads, QK_ROPE))], axis=1
    ).reshape(1, heads * HEAD)
    clipped_q = (query_weight.astype(jnp.float32) * factors).astype(jnp.bfloat16)
    clipped_k = (key_weight.astype(jnp.float32) * jnp.repeat(root, QK_NOPE)[None]).astype(jnp.bfloat16)
    return (attended[None], logit_max, clipped_q, clipped_k)


def solution(mesh):
    fine = Mesh(mesh.devices.reshape(2, 2, 8, 2, 4), ("xh", "core", "z", "xl", "tensor"))
    dp, ctx = ("xh", "core"), ("z", "xl")
    return jax.shard_map(
        local,
        mesh=fine,
        in_specs=(
            P(dp, ctx, None),
            P(dp, ctx, None),
            P(dp, ctx, None),
            P(),
            P(GROUP, "tensor"),
            P(GROUP, "tensor"),
            P(GROUP, "tensor"),
        ),
        out_specs=(
            P(dp, ctx, "tensor"),
            P("tensor"),
            P(GROUP, "tensor"),
            P(GROUP, "tensor"),
        ),
        check_vma=False,
    )
```

```python
import functools
import math

import jax
import jax.numpy as jnp
from jax import lax
from jax.experimental import pallas as pl
from jax.experimental.pallas import tpu as pltpu
from jax.sharding import Mesh
from jax.sharding import PartitionSpec as P

QK_NOPE = 128
QK_ROPE = 64
V_DIM = 128
TAU = 100
HEAD = QK_NOPE + QK_ROPE
SCALE = 1.0 / math.sqrt(HEAD)
SCALE2 = SCALE * math.log2(math.e)
FAR = 1e30

GROUP = ("xh", "core", "z", "xl")
X = ("xh", "xl")
TOK = 512
HALF = TOK // 2
GROUPS_A = (4, 4, 2)
GROUPS_B = (4, 2)
HEADS_A = sum(GROUPS_A)
HEADS_B = sum(GROUPS_B)
WIDE = 3 * HEAD + QK_NOPE + V_DIM
MIB = 1024 * 1024
VMEM = pl.BlockSpec(memory_space=pltpu.VMEM)
SMEM = pl.BlockSpec(memory_space=pltpu.SMEM)
ANY = pl.BlockSpec(memory_space=pl.ANY)


def in_hbm(array):
    return pltpu.with_memory_space_constraint(array, pltpu.HBM)


def whole(shape):
    return pl.BlockSpec(shape, lambda p: (0,) * len(shape))


def dot_f32(a, b):
    return jnp.dot(a, b, preferred_element_type=jnp.float32)


def dot_t(a, b):
    return lax.dot_general(a, b, (((1,), (1,)), ((), ())), preferred_element_type=jnp.float32)


def attend_some(heads, seen, x_ref, lat_ref, rope_ref, weight, wait_query, out_ref, peak_ref):
    at = 3 * heads * HEAD
    keys = dot_f32(lat_ref[...], weight(at, heads * QK_NOPE)).astype(jnp.bfloat16)
    values = dot_f32(lat_ref[...], weight(at + heads * QK_NOPE, heads * V_DIM)).astype(jnp.bfloat16)
    wait_query()
    query = [dot_f32(x_ref[j], weight(j * heads * HEAD, heads * HEAD)) for j in range(3)]
    query = functools.reduce(jnp.add, query).astype(jnp.bfloat16)
    rope = rope_ref[...]
    row = lax.broadcasted_iota(jnp.int32, (HALF, HALF), 0)
    col = lax.broadcasted_iota(jnp.int32, (HALF, HALF), 1)
    diagonal = col <= row
    ones = (lax.broadcasted_iota(jnp.int32, (2 * TOK, V_DIM), 1) == 0).astype(jnp.bfloat16)

    def logits_of(head, part):
        q_part = query[part * HALF : (part + 1) * HALF, head * HEAD : (head + 1) * HEAD]
        key_head = jnp.concatenate([keys[:, head * QK_NOPE : (head + 1) * QK_NOPE], rope], axis=1)
        spans = [(0, HALF, "all")] if part == 1 else []
        spans += [(part * HALF, HALF, "diag"), (TOK, TOK, "prev")]
        logits = []
        for start, size, kind in spans:
            s = dot_t(q_part, key_head[start : start + size])
            logits.append(jnp.where(diagonal, s, -jnp.inf) if kind == "diag" else s)
        return spans, logits

    def finish(head, part, spans, logits):
        value_head = jnp.concatenate([values[:, head * V_DIM : (head + 1) * V_DIM], ones], axis=1)
        peak = functools.reduce(jnp.maximum, [jnp.max(s, axis=1, keepdims=True) for s in logits[:-1]])
        prev_peak = jnp.max(logits[-1], axis=1, keepdims=True)
        peak = jnp.where(seen, jnp.maximum(peak, prev_peak), peak)
        shift = peak * SCALE2
        shift_prev = jnp.where(seen, shift, FAR)
        result = None
        for s, (start, size, kind) in zip(logits, spans):
            expo = jnp.exp2(s * SCALE2 - (shift_prev if kind == "prev" else shift))
            term = dot_f32(expo.astype(jnp.bfloat16), value_head[start : start + size])
            result = term if result is None else result + term
        result = result[:, :V_DIM] * (1.0 / result[:, V_DIM : V_DIM + 1])
        out_ref[part * HALF : (part + 1) * HALF, head * V_DIM : (head + 1) * V_DIM] = result.astype(jnp.bfloat16)
        return jnp.max(peak)

    order = [(head, part) for head in range(heads) for part in range(2)]
    peaks = []
    current = logits_of(*order[0])
    for i, (head, part) in enumerate(order):
        following = logits_of(*order[i + 1]) if i + 1 < len(order) else None
        peaks.append(finish(head, part, *current))
        current = following
    for head in range(heads):
        top = jnp.maximum(peaks[2 * head], peaks[2 * head + 1]) * SCALE
        peak_ref[head : head + 1, :] = jnp.broadcast_to(top, (1, 128))


def from_gathered(place_ref, pieces):
    return [(pieces[0], pl.ds(0, TOK))]


def from_ring(place_ref, pieces):
    me, core = place_ref[1], place_ref[2]
    made = []
    for side in range(2):
        owner = core if side == 0 else 1 - core
        for piece, distance, first in zip(pieces[5 * side : 5 * side + 5], (0, 3, 1, 2, 2), (0, 0, 0, 0, 32)):
            block = lax.rem(me + distance, 4) * 2 + owner
            made.append((piece, pl.ds(pl.multiple_of(block * 64 + first, 32), piece.shape[0])))
    return made


def attend_kernel(rows_of, groups, first, count, away, place_ref, x_ref, lat_ref, rope_ref, *rest):
    pieces = rest[:count]
    out_hbm, peak_ref, w_ref, out_ref, sems, out_sems, own_sems, *own = rest[-10 if away else -7 :]
    rows = rows_of(place_ref, pieces)
    loads = [pltpu.make_async_copy(*pair, own_sems.at[i]) for i, pair in enumerate(zip((x_ref, lat_ref, rope_ref), own))]
    if away:
        x_ref, lat_ref, rope_ref = own
    starts = [sum(groups[:i]) for i in range(len(groups))]

    def copies(group, part):
        heads, start = groups[group], starts[group] * WIDE
        split = 3 * heads * HEAD
        columns = pl.ds(start + split, heads * WIDE - split) if part == 0 else pl.ds(start, split)
        return [
            pltpu.make_async_copy(piece.at[:, columns], w_ref.at[where, columns], sems.at[group, part, i])
            for i, (piece, where) in enumerate(rows)
        ]

    def start(group, parts=(0, 1)):
        for part in parts:
            for copy in copies(group, part):
                copy.start()

    for load in loads[1:]:
        load.start()
    start(0, (0,))
    for load in loads[:1]:
        load.start()
    start(0, (1,))
    results = []
    for group, heads in enumerate(groups):

        def wait(part, group=group):
            for copy in copies(group, part):
                copy.wait()

        def wait_query(group=group, wait=wait):
            for load in loads[:1] if group == 0 else ():
                load.wait()
            wait(1)
            if group + 1 < len(groups):
                start(group + 1)

        def weight(at, width, group=group):
            at = starts[group] * WIDE + at
            return w_ref[:, at : at + width]

        for load in loads[1:] if group == 0 else ():
            load.wait()
        wait(0)
        here = pl.ds(starts[group] * V_DIM, heads * V_DIM)
        out = out_ref.at[:, here]
        peak = peak_ref.at[pl.ds(starts[group], heads), :]
        attend_some(heads, place_ref[0] > 0, x_ref, lat_ref, rope_ref, weight, wait_query, out, peak)
        there = pl.ds((first + starts[group]) * V_DIM, heads * V_DIM)
        results.append(pltpu.make_async_copy(out, out_hbm.at[:, there], out_sems.at[group]))
        results[-1].start()
    for result in results:
        result.wait()


def attend(rows_of, groups, first, name, place, x, latents, rope, pieces, before=()):
    heads, count, away = sum(groups), len(pieces), bool(before)
    own = (x, latents, rope)
    return pl.pallas_call(
        functools.partial(attend_kernel, rows_of, groups, first, count, away),
        in_specs=[SMEM] + [ANY if away else VMEM] * 3 + [ANY] * (count + len(before)),
        out_specs=[ANY, VMEM],
        out_shape=[
            jax.ShapeDtypeStruct((TOK, (HEADS_A + HEADS_B) * V_DIM), jnp.bfloat16),
            jax.ShapeDtypeStruct((16, 128), jnp.float32),
        ],
        input_output_aliases={4 + count: 0} if before else {},
        scratch_shapes=[
            pltpu.VMEM((TOK, heads * WIDE), jnp.bfloat16),
            pltpu.VMEM((TOK, heads * V_DIM), jnp.bfloat16),
            pltpu.SemaphoreType.DMA((len(groups), 2, count)),
            pltpu.SemaphoreType.DMA((len(groups),)),
            pltpu.SemaphoreType.DMA((3,)),
        ]
        + [pltpu.VMEM(a.shape, a.dtype) for a in (own if away else ())],
        compiler_params=pltpu.CompilerParams(vmem_limit_bytes=(40 if away else 24) * MIB),
        cost_estimate=pl.CostEstimate(
            flops=900_000_000 * heads, bytes_accessed=1_000_000 * heads, transcendentals=500_000 * heads
        ),
        name=name,
    )(place, *[in_hbm(a) if away else a for a in own], *pieces, *before)


def pack_kernel(q_ref, k_ref, v_ref, a_ref, b_ref):
    head = 0
    for groups, ref in ((GROUPS_A, a_ref), (GROUPS_B, b_ref)):
        at = 0
        for heads in groups:
            for j in range(3):
                columns = slice(head * HEAD, (head + heads) * HEAD)
                ref[:, at : at + heads * HEAD] = q_ref[8 * j : 8 * j + 8, columns]
                at += heads * HEAD
            for source in (k_ref, v_ref):
                ref[:, at : at + heads * QK_NOPE] = source[:, head * QK_NOPE : (head + heads) * QK_NOPE]
                at += heads * QK_NOPE
            head += heads


def pack(*weights):
    shapes = [jax.ShapeDtypeStruct((8, heads * WIDE), jnp.bfloat16) for heads in (HEADS_A, HEADS_B)]
    return pl.pallas_call(
        pack_kernel,
        grid=(1,),
        in_specs=[whole(a.shape) for a in weights],
        out_specs=[whole(a.shape) for a in shapes],
        out_shape=shapes,
        compiler_params=pltpu.CompilerParams(vmem_limit_bytes=8 * MIB),
        name="pack",
    )(*[in_hbm(a) for a in weights])


def order_kernel(offsets, me_ref, *refs):
    pieces, out_ref = refs[:-1], refs[-1]
    count = len(pieces)
    for offset, piece in zip(offsets, pieces):
        out_ref[lax.rem(me_ref[0] + offset % count, count)] = piece[...]


def in_order(me, offsets, pieces):
    rows, columns = pieces[0].shape
    count = len(pieces)
    return pl.pallas_call(
        functools.partial(order_kernel, offsets),
        in_specs=[SMEM] + [VMEM] * count,
        out_specs=VMEM,
        out_shape=jax.ShapeDtypeStruct((count, rows, columns), jnp.bfloat16),
        compiler_params=pltpu.CompilerParams(vmem_limit_bytes=4 * MIB),
        name="in_order",
    )(me.reshape(1), *pieces).reshape(count * rows, columns)


def halves_kernel(before_ref, after_ref, low_ref, high_ref):
    low_ref[...] = before_ref[:32]
    high_ref[...] = after_ref[32:]


def halves(before, after):
    shape = jax.ShapeDtypeStruct((32, before.shape[1]), before.dtype)
    return pl.pallas_call(
        halves_kernel,
        in_specs=[VMEM] * 2,
        out_specs=[VMEM] * 2,
        out_shape=[shape, shape],
        compiler_params=pltpu.CompilerParams(vmem_limit_bytes=4 * MIB),
        name="halves",
    )(before, after)


def one_hot(source, first):
    at = lax.broadcasted_iota(jnp.int32, (128, source.shape[1]), 0) + first
    return jnp.where(at == source, 1.0, 0.0).astype(jnp.bfloat16)


def picked(rows, tiles, source):
    left = jnp.concatenate([rows(tile) for tile in tiles], axis=1)
    right = jnp.concatenate([one_hot(source, tile * 128) for tile in tiles], axis=0)
    return dot_f32(left, right).astype(jnp.bfloat16)


def late_source(c, tile, strip):
    z, core, xh, xl, r = 2 * tile + ((c >> 6) & 1), (c >> 5) & 1, (c >> 4) & 1, (c >> 3) & 1, c & 7
    return ((xh * 2 + core) * 16 + z * 2 + xl) * strip + r


def early_source(c, tile, strip):
    core, z, r = (c >> 6) & 1, (c >> 3) & 7, c & 7
    return ((tile // 2 * 2 + core) * 16 + z * 2 + tile % 2) * strip + r


def order_query_kernel(x_ref, late_ref, early_ref):
    column = lax.broadcasted_iota(jnp.int32, (1, 384), 1)
    c, j = column & 127, column >> 7
    rows = lambda tile: x_ref[:, tile * 128 : (tile + 1) * 128]
    for tile in range(4):
        low, high = 96 * tile // 128, (96 * tile + 95) // 128
        near = [3 * block + part for block in range(4) for part in range(low, high + 1)]
        late = picked(rows, near, late_source(c, tile, 24) + 8 * j)
        near = [3 * (tile // 2 * 2 + core) + part for core in range(2) for part in range(3)]
        early = picked(rows, near, early_source(c, tile, 24) + 8 * j)
        for strip in range(3):
            late_ref[strip, :, tile * 128 : (tile + 1) * 128] = late[:, strip * 128 : (strip + 1) * 128]
            early_ref[strip, :, tile * 128 : (tile + 1) * 128] = early[:, strip * 128 : (strip + 1) * 128]


def order_query(x):
    shape = jax.ShapeDtypeStruct((3, TOK, 512), jnp.bfloat16)
    return pl.pallas_call(
        order_query_kernel,
        grid=(1,),
        in_specs=[whole(x.shape)],
        out_specs=[whole(shape.shape)] * 2,
        out_shape=[shape, shape],
        compiler_params=pltpu.CompilerParams(vmem_limit_bytes=16 * MIB),
        cost_estimate=pl.CostEstimate(flops=2_500_000_000, bytes_accessed=6_000_000, transcendentals=0),
        name="order_query",
    )(x)


def order_latent_kernel(me_ref, own_ref, own_rope_ref, *refs):
    pieces, (late_ref, early_ref, rope_ref, prev_ref) = refs[:4], refs[4:]
    for offset, piece in zip((0, -1, 1, 2), pieces):
        slot = lax.rem(me_ref[0] + offset % 4, 4)
        prev_ref[pl.ds(pl.multiple_of(slot * 128, 128), 128), :] = piece[...]
    rope_ref[:TOK] = own_rope_ref[...]
    rope_ref[TOK:] = prev_ref[:, 512:]
    c = lax.broadcasted_iota(jnp.int32, (1, 128), 1)
    for part, ref in ((0, own_ref), (1, prev_ref)):
        rows = lambda tile: ref[:, tile * 128 : (tile + 1) * 128]
        for tile in range(4):
            at = slice(tile * 128, (tile + 1) * 128)
            late_ref[part * TOK : (part + 1) * TOK, at] = picked(rows, range(4), late_source(c, tile, 8))
            near = [tile // 2 * 2, tile // 2 * 2 + 1]
            early_ref[part * TOK : (part + 1) * TOK, at] = picked(rows, near, early_source(c, tile, 8))


def order_latent(me, own, own_rope, pieces):
    operands = (own, own_rope, *pieces)
    shapes = [jax.ShapeDtypeStruct((2 * TOK, width), jnp.bfloat16) for width in (512, 512, QK_ROPE)]
    return pl.pallas_call(
        order_latent_kernel,
        grid=(1,),
        in_specs=[SMEM] + [whole(a.shape) for a in operands],
        out_specs=[whole(a.shape) for a in shapes],
        out_shape=shapes,
        scratch_shapes=[pltpu.VMEM((TOK, 512 + QK_ROPE), jnp.bfloat16)],
        compiler_params=pltpu.CompilerParams(vmem_limit_bytes=16 * MIB),
        cost_estimate=pl.CostEstimate(flops=1_000_000_000, bytes_accessed=4_000_000, transcendentals=0),
        name="order_latent",
    )(me.reshape(1), *operands)


def moved(block, axes, distance):
    count = lax.axis_size(axes)
    return lax.ppermute(block, axes, [(i, (i + distance) % count) for i in range(count)])


def local(query_latent, shared_latent, rope_keys, block_order, query_weight, key_weight, value_weight):
    heads = key_weight.shape[1] // QK_NOPE
    me_x = lax.axis_index(X).astype(jnp.int32)
    me_z = lax.axis_index("z").astype(jnp.int32)
    me_core = lax.axis_index("core").astype(jnp.int32)
    cycle = lax.axis_size(("z", "xl"))
    packed_a, packed_b = pack(query_weight, key_weight, value_weight)

    barrier = lax.optimization_barrier
    me_t = lax.axis_index("tensor").astype(jnp.int32)
    quarter = TOK // lax.axis_size("tensor")

    along_x = [packed_a, moved(packed_a, X, 1), moved(packed_a, X, -1), moved(packed_a, X, 2)]
    shard_a = in_order(me_x, (0, -1, 1, 2), along_x)
    shard_a, latent, rope_own, block_order = barrier((shard_a, shared_latent[0], rope_keys[0], block_order))
    gathered_a = lax.all_gather(shard_a, ("z", "core"), axis=0, tiled=True)

    position = lax.axis_index(("z", "xl"))
    order_row = block_order[lax.axis_index(("xh", "core"))]
    seen = (order_row[(position - 1 + cycle) % cycle] < order_row[position]).astype(jnp.int32)
    place = jnp.stack([seen, me_x, me_core])
    mine = jnp.concatenate(
        [lax.dynamic_slice_in_dim(a, me_t * quarter, quarter, 0) for a in (latent, rope_own)], axis=1
    )
    up, down = moved(packed_b, "z", 1), moved(packed_b, "z", -1)
    up2, down2 = moved(packed_b, "z", 2), moved(packed_b, "z", -2)
    up3, down3, up4 = moved(up2, "z", 1), moved(down2, "z", -1), moved(up2, "z", 2)
    own = in_order(me_z, (0, -1, 1, -2, 2, -3, 3, -4), [packed_b, up, down, up2, down2, up3, down3, up4])
    theirs = moved(mine, ("z", "xl"), 1)
    own, theirs, place, rope_own = barrier((own, theirs, place, rope_own))

    before, after = moved(own, X, 1), moved(own, X, -1)
    prev = [theirs, moved(theirs, "tensor", 1), moved(theirs, "tensor", -1), moved(theirs, "tensor", 2)]
    x_a, x_b = order_query(query_latent[0])
    before, after, x_a, x_b = barrier((before, after, x_a, x_b))
    low, high = halves(before, after)
    far_low, far_high = moved(low, X, 1), moved(high, X, -1)
    lat_a, lat_b, rope = order_latent(me_t, latent, rope_own, prev)
    far_low, far_high, lat_a, lat_b, rope = barrier((far_low, far_high, lat_a, lat_b, rope))
    mine = [own, before, after, far_low, far_high]
    pieces = mine + [moved(piece, "core", 1) for piece in mine]

    out, peaks_b = attend(from_ring, GROUPS_B, HEADS_A, "ringed", place, x_b, lat_b, rope, pieces)
    gathered_a = [in_hbm(gathered_a)]
    attended, peaks_a = attend(from_gathered, GROUPS_A, 0, "gathered", place, x_a, lat_a, rope, gathered_a, [out])

    peaks = jnp.concatenate([peaks_a[:HEADS_A, 0], peaks_b[:HEADS_B, 0]]).reshape(1, heads)
    everyone = lax.axis_size(GROUP)
    shared = lax.all_to_all(jnp.broadcast_to(peaks[None], (everyone, 1, heads)), GROUP, 0, 0)
    logit_max = jnp.max(shared, axis=(0, 1))
    clip = TAU / jnp.maximum(logit_max, TAU)
    root = jnp.sqrt(clip)
    factors = jnp.concatenate(
        [jnp.broadcast_to(root[:, None], (heads, QK_NOPE)), jnp.broadcast_to(clip[:, None], (heads, QK_ROPE))], axis=1
    ).reshape(1, heads * HEAD)
    clipped_q = (query_weight.astype(jnp.float32) * factors).astype(jnp.bfloat16)
    clipped_k = (key_weight.astype(jnp.float32) * jnp.repeat(root, QK_NOPE)[None]).astype(jnp.bfloat16)
    return (attended[None], logit_max, clipped_q, clipped_k)


def solution(mesh):
    fine = Mesh(mesh.devices.reshape(2, 2, 8, 2, 4), ("xh", "core", "z", "xl", "tensor"))
    dp, ctx = ("xh", "core"), ("z", "xl")
    return jax.shard_map(
        local,
        mesh=fine,
        in_specs=(
            P(dp, ctx, None),
            P(dp, ctx, None),
            P(dp, ctx, None),
            P(),
            P(GROUP, "tensor"),
            P(GROUP, "tensor"),
            P(GROUP, "tensor"),
        ),
        out_specs=(
            P(dp, ctx, "tensor"),
            P("tensor"),
            P(GROUP, "tensor"),
            P(GROUP, "tensor"),
        ),
        check_vma=False,
    )
```

```python
import functools
import math

import jax
import jax.numpy as jnp
from jax import lax
from jax.experimental import pallas as pl
from jax.experimental.pallas import tpu as pltpu
from jax.sharding import Mesh
from jax.sharding import PartitionSpec as P

QK_NOPE = 128
QK_ROPE = 64
V_DIM = 128
TAU = 100
HEAD = QK_NOPE + QK_ROPE
SCALE = 1.0 / math.sqrt(HEAD)
SCALE2 = SCALE * math.log2(math.e)
FAR = 1e30

GROUP = ("xh", "core", "z", "xl")
X = ("xh", "xl")
TOK = 512
HALF = TOK // 2
GROUPS_A = (2,) * 5
GROUPS_B = (2,) * 3
HEADS_A = sum(GROUPS_A)
HEADS_B = sum(GROUPS_B)
WIDE = 3 * HEAD + QK_NOPE + V_DIM
MIB = 1024 * 1024
VMEM = pl.BlockSpec(memory_space=pltpu.VMEM)
SMEM = pl.BlockSpec(memory_space=pltpu.SMEM)
ANY = pl.BlockSpec(memory_space=pl.ANY)


def in_hbm(array):
    return pltpu.with_memory_space_constraint(array, pltpu.HBM)


def whole(shape):
    return pl.BlockSpec(shape, lambda p: (0,) * len(shape))


def dot_f32(a, b):
    return jnp.dot(a, b, preferred_element_type=jnp.float32)


def dot_t(a, b):
    return lax.dot_general(a, b, (((1,), (1,)), ((), ())), preferred_element_type=jnp.float32)


def attend_some(heads, seen, x_ref, lat_ref, rope_ref, weight, out_ref, peak_ref):
    query = [dot_f32(x_ref[j], weight(j * heads * HEAD, heads * HEAD)) for j in range(3)]
    query = functools.reduce(jnp.add, query).astype(jnp.bfloat16)
    at = 3 * heads * HEAD
    keys = dot_f32(lat_ref[...], weight(at, heads * QK_NOPE)).astype(jnp.bfloat16)
    values = dot_f32(lat_ref[...], weight(at + heads * QK_NOPE, heads * V_DIM)).astype(jnp.bfloat16)
    rope = rope_ref[...]
    row = lax.broadcasted_iota(jnp.int32, (HALF, HALF), 0)
    col = lax.broadcasted_iota(jnp.int32, (HALF, HALF), 1)
    diagonal = col <= row
    ones = (lax.broadcasted_iota(jnp.int32, (2 * TOK, V_DIM), 1) == 0).astype(jnp.bfloat16)

    def logits_of(head, part):
        q_part = query[part * HALF : (part + 1) * HALF, head * HEAD : (head + 1) * HEAD]
        key_head = jnp.concatenate([keys[:, head * QK_NOPE : (head + 1) * QK_NOPE], rope], axis=1)
        spans = [(0, HALF, "all")] if part == 1 else []
        spans += [(part * HALF, HALF, "diag"), (TOK, TOK, "prev")]
        logits = []
        for start, size, kind in spans:
            s = dot_t(q_part, key_head[start : start + size])
            logits.append(jnp.where(diagonal, s, -jnp.inf) if kind == "diag" else s)
        return spans, logits

    def finish(head, part, spans, logits):
        value_head = jnp.concatenate([values[:, head * V_DIM : (head + 1) * V_DIM], ones], axis=1)
        peak = functools.reduce(jnp.maximum, [jnp.max(s, axis=1, keepdims=True) for s in logits[:-1]])
        prev_peak = jnp.max(logits[-1], axis=1, keepdims=True)
        peak = jnp.where(seen, jnp.maximum(peak, prev_peak), peak)
        shift = peak * SCALE2
        shift_prev = jnp.where(seen, shift, FAR)
        result = None
        for s, (start, size, kind) in zip(logits, spans):
            expo = jnp.exp2(s * SCALE2 - (shift_prev if kind == "prev" else shift))
            term = dot_f32(expo.astype(jnp.bfloat16), value_head[start : start + size])
            result = term if result is None else result + term
        result = result[:, :V_DIM] * (1.0 / result[:, V_DIM : V_DIM + 1])
        out_ref[part * HALF : (part + 1) * HALF, head * V_DIM : (head + 1) * V_DIM] = result.astype(jnp.bfloat16)
        return jnp.max(peak)

    order = [(head, part) for head in range(heads) for part in range(2)]
    peaks = []
    current = logits_of(*order[0])
    for i, (head, part) in enumerate(order):
        following = logits_of(*order[i + 1]) if i + 1 < len(order) else None
        peaks.append(finish(head, part, *current))
        current = following
    for head in range(heads):
        top = jnp.maximum(peaks[2 * head], peaks[2 * head + 1]) * SCALE
        peak_ref[head : head + 1, :] = jnp.broadcast_to(top, (1, 128))


def from_gathered(place_ref, pieces):
    return [(pieces[0], pl.ds(0, TOK))]


def from_ring(place_ref, pieces):
    me, core = place_ref[1], place_ref[2]
    made = []
    for side in range(2):
        owner = core if side == 0 else 1 - core
        for piece, distance, first in zip(pieces[5 * side : 5 * side + 5], (0, 3, 1, 2, 2), (0, 0, 0, 0, 32)):
            block = lax.rem(me + distance, 4) * 2 + owner
            made.append((piece, pl.ds(pl.multiple_of(block * 64 + first, 32), piece.shape[0])))
    return made


def attend_kernel(rows_of, heads, steps, count, away, place_ref, x_ref, lat_ref, rope_ref, *rest):
    pieces = rest[:count]
    out_ref, peak_ref, w_ref, sems, own_sems, *own = rest[-8 if away else -5 :]
    rows = rows_of(place_ref, pieces)
    loads = [pltpu.make_async_copy(*pair, own_sems.at[i]) for i, pair in enumerate(zip((x_ref, lat_ref, rope_ref), own))]
    if away:
        x_ref, lat_ref, rope_ref = own
    step = pl.program_id(0)
    slot = lax.rem(step, 2)
    wide = heads * WIDE

    def copies(step, slot):
        columns = pl.ds(pl.multiple_of(step * wide, 128), wide)
        return [
            pltpu.make_async_copy(piece.at[:, columns], w_ref.at[slot, where], sems.at[slot, i])
            for i, (piece, where) in enumerate(rows)
        ]

    @pl.when(step == 0)
    def _():
        for copy in [*loads, *copies(0, 0)]:
            copy.start()
        for load in loads:
            load.wait()

    for copy in copies(step, slot):
        copy.wait()

    @pl.when(step + 1 < steps)
    def _():
        for copy in copies(step + 1, 1 - slot):
            copy.start()

    weight = lambda at, width: w_ref[slot, :, at : at + width]
    attend_some(heads, place_ref[0] > 0, x_ref, lat_ref, rope_ref, weight, out_ref, peak_ref.at[0])


def attend(rows_of, groups, first, name, place, x, latents, rope, pieces, before=()):
    heads, steps, count, away = groups[0], len(groups), len(pieces), bool(before)
    own = (x, latents, rope)
    return pl.pallas_call(
        functools.partial(attend_kernel, rows_of, heads, steps, count, away),
        grid=(steps,),
        in_specs=[SMEM] + [ANY if away else VMEM] * 3 + [ANY] * (count + len(before)),
        out_specs=[
            pl.BlockSpec((TOK, heads * V_DIM), lambda p: (0, first // heads + p)),
            pl.BlockSpec((1, 8, 128), lambda p: (p, 0, 0)),
        ],
        out_shape=[
            jax.ShapeDtypeStruct((TOK, (HEADS_A + HEADS_B) * V_DIM), jnp.bfloat16),
            jax.ShapeDtypeStruct((steps, 8, 128), jnp.float32),
        ],
        input_output_aliases={4 + count: 0} if before else {},
        scratch_shapes=[
            pltpu.VMEM((2, TOK, heads * WIDE), jnp.bfloat16),
            pltpu.SemaphoreType.DMA((2, count)),
            pltpu.SemaphoreType.DMA((3,)),
        ]
        + [pltpu.VMEM(a.shape, a.dtype) for a in (own if away else ())],
        compiler_params=pltpu.CompilerParams(vmem_limit_bytes=20 * MIB),
        cost_estimate=pl.CostEstimate(
            flops=900_000_000 * heads * steps,
            bytes_accessed=1_000_000 * heads * steps,
            transcendentals=500_000 * heads * steps,
        ),
        name=name,
    )(place, *[in_hbm(a) if away else a for a in own], *pieces, *before)


def pack_kernel(q_ref, k_ref, v_ref, a_ref, b_ref):
    head = 0
    for groups, ref in ((GROUPS_A, a_ref), (GROUPS_B, b_ref)):
        at = 0
        for heads in groups:
            for j in range(3):
                columns = slice(head * HEAD, (head + heads) * HEAD)
                ref[:, at : at + heads * HEAD] = q_ref[8 * j : 8 * j + 8, columns]
                at += heads * HEAD
            for source in (k_ref, v_ref):
                ref[:, at : at + heads * QK_NOPE] = source[:, head * QK_NOPE : (head + heads) * QK_NOPE]
                at += heads * QK_NOPE
            head += heads


def pack(*weights):
    shapes = [jax.ShapeDtypeStruct((8, heads * WIDE), jnp.bfloat16) for heads in (HEADS_A, HEADS_B)]
    return pl.pallas_call(
        pack_kernel,
        grid=(1,),
        in_specs=[whole(a.shape) for a in weights],
        out_specs=[whole(a.shape) for a in shapes],
        out_shape=shapes,
        compiler_params=pltpu.CompilerParams(vmem_limit_bytes=8 * MIB),
        name="pack",
    )(*[in_hbm(a) for a in weights])


def order_kernel(offsets, me_ref, *refs):
    pieces, out_ref = refs[:-1], refs[-1]
    count = len(pieces)
    for offset, piece in zip(offsets, pieces):
        out_ref[lax.rem(me_ref[0] + offset % count, count)] = piece[...]


def in_order(me, offsets, pieces):
    rows, columns = pieces[0].shape
    count = len(pieces)
    return pl.pallas_call(
        functools.partial(order_kernel, offsets),
        in_specs=[SMEM] + [VMEM] * count,
        out_specs=VMEM,
        out_shape=jax.ShapeDtypeStruct((count, rows, columns), jnp.bfloat16),
        compiler_params=pltpu.CompilerParams(vmem_limit_bytes=4 * MIB),
        name="in_order",
    )(me.reshape(1), *pieces).reshape(count * rows, columns)


def halves_kernel(before_ref, after_ref, low_ref, high_ref):
    low_ref[...] = before_ref[:32]
    high_ref[...] = after_ref[32:]


def halves(before, after):
    shape = jax.ShapeDtypeStruct((32, before.shape[1]), before.dtype)
    return pl.pallas_call(
        halves_kernel,
        in_specs=[VMEM] * 2,
        out_specs=[VMEM] * 2,
        out_shape=[shape, shape],
        compiler_params=pltpu.CompilerParams(vmem_limit_bytes=4 * MIB),
        name="halves",
    )(before, after)


def one_hot(source, first):
    at = lax.broadcasted_iota(jnp.int32, (128, source.shape[1]), 0) + first
    return jnp.where(at == source, 1.0, 0.0).astype(jnp.bfloat16)


def picked(rows, tiles, source):
    left = jnp.concatenate([rows(tile) for tile in tiles], axis=1)
    right = jnp.concatenate([one_hot(source, tile * 128) for tile in tiles], axis=0)
    return dot_f32(left, right).astype(jnp.bfloat16)


def late_source(c, tile, strip):
    z, core, xh, xl, r = 2 * tile + ((c >> 6) & 1), (c >> 5) & 1, (c >> 4) & 1, (c >> 3) & 1, c & 7
    return ((xh * 2 + core) * 16 + z * 2 + xl) * strip + r


def early_source(c, tile, strip):
    core, z, r = (c >> 6) & 1, (c >> 3) & 7, c & 7
    return ((tile // 2 * 2 + core) * 16 + z * 2 + tile % 2) * strip + r


def order_query_kernel(x_ref, late_ref, early_ref):
    column = lax.broadcasted_iota(jnp.int32, (1, 384), 1)
    c, j = column & 127, column >> 7
    rows = lambda tile: x_ref[:, tile * 128 : (tile + 1) * 128]
    for tile in range(4):
        low, high = 96 * tile // 128, (96 * tile + 95) // 128
        near = [3 * block + part for block in range(4) for part in range(low, high + 1)]
        late = picked(rows, near, late_source(c, tile, 24) + 8 * j)
        near = [3 * (tile // 2 * 2 + core) + part for core in range(2) for part in range(3)]
        early = picked(rows, near, early_source(c, tile, 24) + 8 * j)
        for strip in range(3):
            late_ref[strip, :, tile * 128 : (tile + 1) * 128] = late[:, strip * 128 : (strip + 1) * 128]
            early_ref[strip, :, tile * 128 : (tile + 1) * 128] = early[:, strip * 128 : (strip + 1) * 128]


def order_query(x):
    shape = jax.ShapeDtypeStruct((3, TOK, 512), jnp.bfloat16)
    return pl.pallas_call(
        order_query_kernel,
        grid=(1,),
        in_specs=[whole(x.shape)],
        out_specs=[whole(shape.shape)] * 2,
        out_shape=[shape, shape],
        compiler_params=pltpu.CompilerParams(vmem_limit_bytes=16 * MIB),
        cost_estimate=pl.CostEstimate(flops=2_500_000_000, bytes_accessed=6_000_000, transcendentals=0),
        name="order_query",
    )(x)


def order_latent_kernel(me_ref, own_ref, own_rope_ref, *refs):
    pieces, (late_ref, early_ref, rope_ref, prev_ref) = refs[:4], refs[4:]
    for offset, piece in zip((0, -1, 1, 2), pieces):
        slot = lax.rem(me_ref[0] + offset % 4, 4)
        prev_ref[pl.ds(pl.multiple_of(slot * 128, 128), 128), :] = piece[...]
    rope_ref[:TOK] = own_rope_ref[...]
    rope_ref[TOK:] = prev_ref[:, 512:]
    c = lax.broadcasted_iota(jnp.int32, (1, 128), 1)
    for part, ref in ((0, own_ref), (1, prev_ref)):
        rows = lambda tile: ref[:, tile * 128 : (tile + 1) * 128]
        for tile in range(4):
            at = slice(tile * 128, (tile + 1) * 128)
            late_ref[part * TOK : (part + 1) * TOK, at] = picked(rows, range(4), late_source(c, tile, 8))
            near = [tile // 2 * 2, tile // 2 * 2 + 1]
            early_ref[part * TOK : (part + 1) * TOK, at] = picked(rows, near, early_source(c, tile, 8))


def order_latent(me, own, own_rope, pieces):
    operands = (own, own_rope, *pieces)
    shapes = [jax.ShapeDtypeStruct((2 * TOK, width), jnp.bfloat16) for width in (512, 512, QK_ROPE)]
    return pl.pallas_call(
        order_latent_kernel,
        grid=(1,),
        in_specs=[SMEM] + [whole(a.shape) for a in operands],
        out_specs=[whole(a.shape) for a in shapes],
        out_shape=shapes,
        scratch_shapes=[pltpu.VMEM((TOK, 512 + QK_ROPE), jnp.bfloat16)],
        compiler_params=pltpu.CompilerParams(vmem_limit_bytes=16 * MIB),
        cost_estimate=pl.CostEstimate(flops=1_000_000_000, bytes_accessed=4_000_000, transcendentals=0),
        name="order_latent",
    )(me.reshape(1), *operands)


def moved(block, axes, distance):
    count = lax.axis_size(axes)
    return lax.ppermute(block, axes, [(i, (i + distance) % count) for i in range(count)])


def local(query_latent, shared_latent, rope_keys, block_order, query_weight, key_weight, value_weight):
    heads = key_weight.shape[1] // QK_NOPE
    me_x = lax.axis_index(X).astype(jnp.int32)
    me_z = lax.axis_index("z").astype(jnp.int32)
    me_core = lax.axis_index("core").astype(jnp.int32)
    cycle = lax.axis_size(("z", "xl"))
    packed_a, packed_b = pack(query_weight, key_weight, value_weight)

    barrier = lax.optimization_barrier
    me_t = lax.axis_index("tensor").astype(jnp.int32)
    quarter = TOK // lax.axis_size("tensor")

    along_x = [packed_a, moved(packed_a, X, 1), moved(packed_a, X, -1), moved(packed_a, X, 2)]
    shard_a = in_order(me_x, (0, -1, 1, 2), along_x)
    shard_a, latent, rope_own, block_order = barrier((shard_a, shared_latent[0], rope_keys[0], block_order))
    gathered_a = lax.all_gather(shard_a, ("z", "core"), axis=0, tiled=True)

    position = lax.axis_index(("z", "xl"))
    order_row = block_order[lax.axis_index(("xh", "core"))]
    seen = (order_row[(position - 1 + cycle) % cycle] < order_row[position]).astype(jnp.int32)
    place = jnp.stack([seen, me_x, me_core])
    mine = jnp.concatenate(
        [lax.dynamic_slice_in_dim(a, me_t * quarter, quarter, 0) for a in (latent, rope_own)], axis=1
    )
    up, down = moved(packed_b, "z", 1), moved(packed_b, "z", -1)
    up2, down2 = moved(packed_b, "z", 2), moved(packed_b, "z", -2)
    up3, down3, up4 = moved(up2, "z", 1), moved(down2, "z", -1), moved(up2, "z", 2)
    own = in_order(me_z, (0, -1, 1, -2, 2, -3, 3, -4), [packed_b, up, down, up2, down2, up3, down3, up4])
    theirs = moved(mine, ("z", "xl"), 1)
    own, theirs, place, rope_own = barrier((own, theirs, place, rope_own))

    before, after = moved(own, X, 1), moved(own, X, -1)
    prev = [theirs, moved(theirs, "tensor", 1), moved(theirs, "tensor", -1), moved(theirs, "tensor", 2)]
    x_a, x_b = order_query(query_latent[0])
    before, after, x_a, x_b = barrier((before, after, x_a, x_b))
    low, high = halves(before, after)
    far_low, far_high = moved(low, X, 1), moved(high, X, -1)
    lat_a, lat_b, rope = order_latent(me_t, latent, rope_own, prev)
    far_low, far_high, lat_a, lat_b, rope = barrier((far_low, far_high, lat_a, lat_b, rope))
    mine = [own, before, after, far_low, far_high]
    pieces = mine + [moved(piece, "core", 1) for piece in mine]

    out, peaks_b = attend(from_ring, GROUPS_B, HEADS_A, "ringed", place, x_b, lat_b, rope, pieces)
    gathered_a = [in_hbm(gathered_a)]
    attended, peaks_a = attend(from_gathered, GROUPS_A, 0, "gathered", place, x_a, lat_a, rope, gathered_a, [out])

    peaks = jnp.concatenate([peaks_a, peaks_b])[:, : GROUPS_A[0], 0].reshape(1, heads)
    everyone = lax.axis_size(GROUP)
    shared = lax.all_to_all(jnp.broadcast_to(peaks[None], (everyone, 1, heads)), GROUP, 0, 0)
    logit_max = jnp.max(shared, axis=(0, 1))
    clip = TAU / jnp.maximum(logit_max, TAU)
    root = jnp.sqrt(clip)
    factors = jnp.concatenate(
        [jnp.broadcast_to(root[:, None], (heads, QK_NOPE)), jnp.broadcast_to(clip[:, None], (heads, QK_ROPE))], axis=1
    ).reshape(1, heads * HEAD)
    clipped_q = (query_weight.astype(jnp.float32) * factors).astype(jnp.bfloat16)
    clipped_k = (key_weight.astype(jnp.float32) * jnp.repeat(root, QK_NOPE)[None]).astype(jnp.bfloat16)
    return (attended[None], logit_max, clipped_q, clipped_k)


def solution(mesh):
    fine = Mesh(mesh.devices.reshape(2, 2, 8, 2, 4), ("xh", "core", "z", "xl", "tensor"))
    dp, ctx = ("xh", "core"), ("z", "xl")
    return jax.shard_map(
        local,
        mesh=fine,
        in_specs=(
            P(dp, ctx, None),
            P(dp, ctx, None),
            P(dp, ctx, None),
            P(),
            P(GROUP, "tensor"),
            P(GROUP, "tensor"),
            P(GROUP, "tensor"),
        ),
        out_specs=(
            P(dp, ctx, "tensor"),
            P("tensor"),
            P(GROUP, "tensor"),
            P(GROUP, "tensor"),
        ),
        check_vma=False,
    )
```

```python
import functools
import math

import jax
import jax.numpy as jnp
from jax import lax
from jax.experimental import pallas as pl
from jax.experimental.pallas import tpu as pltpu
from jax.sharding import Mesh
from jax.sharding import PartitionSpec as P

QK_NOPE = 128
QK_ROPE = 64
V_DIM = 128
TAU = 100
HEAD = QK_NOPE + QK_ROPE
SCALE = 1.0 / math.sqrt(HEAD)
SCALE2 = SCALE * math.log2(math.e)
FAR = 1e30

GROUP = ("xh", "core", "z", "xl")
X = ("xh", "xl")
TOK = 512
HALF = TOK // 2
GROUPS_A = (2,) * 5
GROUPS_B = (2,) * 3
HEADS_A = sum(GROUPS_A)
HEADS_B = sum(GROUPS_B)
WIDE = 3 * HEAD + QK_NOPE + V_DIM
MIB = 1024 * 1024
VMEM = pl.BlockSpec(memory_space=pltpu.VMEM)
SMEM = pl.BlockSpec(memory_space=pltpu.SMEM)
ANY = pl.BlockSpec(memory_space=pl.ANY)


def in_hbm(array):
    return pltpu.with_memory_space_constraint(array, pltpu.HBM)


def whole(shape):
    return pl.BlockSpec(shape, lambda p: (0,) * len(shape))


def dot_f32(a, b):
    return jnp.dot(a, b, preferred_element_type=jnp.float32)


def dot_t(a, b):
    return lax.dot_general(a, b, (((1,), (1,)), ((), ())), preferred_element_type=jnp.float32)


def attend_some(heads, seen, x_ref, lat_ref, rope_ref, weight, out_ref, peak_ref):
    query = [dot_f32(x_ref[j], weight(j * heads * HEAD, heads * HEAD)) for j in range(3)]
    query = functools.reduce(jnp.add, query).astype(jnp.bfloat16)
    at = 3 * heads * HEAD
    keys = dot_f32(lat_ref[...], weight(at, heads * QK_NOPE)).astype(jnp.bfloat16)
    values = dot_f32(lat_ref[...], weight(at + heads * QK_NOPE, heads * V_DIM)).astype(jnp.bfloat16)
    rope = rope_ref[...]
    row = lax.broadcasted_iota(jnp.int32, (HALF, HALF), 0)
    col = lax.broadcasted_iota(jnp.int32, (HALF, HALF), 1)
    diagonal = col <= row
    ones = (lax.broadcasted_iota(jnp.int32, (2 * TOK, V_DIM), 1) == 0).astype(jnp.bfloat16)

    def logits_of(head, part):
        q_part = query[part * HALF : (part + 1) * HALF, head * HEAD : (head + 1) * HEAD]
        key_head = jnp.concatenate([keys[:, head * QK_NOPE : (head + 1) * QK_NOPE], rope], axis=1)
        spans = [(0, HALF, "all")] if part == 1 else []
        spans += [(part * HALF, HALF, "diag"), (TOK, TOK, "prev")]
        logits = []
        for start, size, kind in spans:
            s = dot_t(q_part, key_head[start : start + size])
            logits.append(jnp.where(diagonal, s, -jnp.inf) if kind == "diag" else s)
        return spans, logits

    def finish(head, part, spans, logits):
        value_head = jnp.concatenate([values[:, head * V_DIM : (head + 1) * V_DIM], ones], axis=1)
        peak = functools.reduce(jnp.maximum, [jnp.max(s, axis=1, keepdims=True) for s in logits[:-1]])
        prev_peak = jnp.max(logits[-1], axis=1, keepdims=True)
        peak = jnp.where(seen, jnp.maximum(peak, prev_peak), peak)
        shift = peak * SCALE2
        shift_prev = jnp.where(seen, shift, FAR)
        result = None
        for s, (start, size, kind) in zip(logits, spans):
            expo = jnp.exp2(s * SCALE2 - (shift_prev if kind == "prev" else shift))
            term = dot_f32(expo.astype(jnp.bfloat16), value_head[start : start + size])
            result = term if result is None else result + term
        result = result[:, :V_DIM] * (1.0 / result[:, V_DIM : V_DIM + 1])
        out_ref[part * HALF : (part + 1) * HALF, head * V_DIM : (head + 1) * V_DIM] = result.astype(jnp.bfloat16)
        return jnp.max(peak)

    order = [(head, part) for head in range(heads) for part in range(2)]
    peaks = []
    current = logits_of(*order[0])
    for i, (head, part) in enumerate(order):
        following = logits_of(*order[i + 1]) if i + 1 < len(order) else None
        peaks.append(finish(head, part, *current))
        current = following
    for head in range(heads):
        top = jnp.maximum(peaks[2 * head], peaks[2 * head + 1]) * SCALE
        peak_ref[head : head + 1, :] = jnp.broadcast_to(top, (1, 128))


def from_gathered(place_ref, pieces):
    return [(pieces[0], pl.ds(0, TOK))]


def from_ring(place_ref, pieces):
    me, core = place_ref[1], place_ref[2]
    made = []
    for side in range(2):
        owner = core if side == 0 else 1 - core
        for piece, distance, first in zip(pieces[5 * side : 5 * side + 5], (0, 3, 1, 2, 2), (0, 0, 0, 0, 32)):
            block = lax.rem(me + distance, 4) * 2 + owner
            made.append((piece, pl.ds(pl.multiple_of(block * 64 + first, 32), piece.shape[0])))
    return made


def attend_kernel(rows_of, heads, steps, count, away, place_ref, x_ref, lat_ref, rope_ref, *rest):
    pieces = rest[:count]
    out_ref, peak_ref, w_ref, sems, own_sems, *own = rest[-8 if away else -5 :]
    rows = rows_of(place_ref, pieces)
    loads = [pltpu.make_async_copy(*pair, own_sems.at[i]) for i, pair in enumerate(zip((x_ref, lat_ref, rope_ref), own))]
    if away:
        x_ref, lat_ref, rope_ref = own
    step = pl.program_id(0)
    slot = lax.rem(step, 2)
    wide = heads * WIDE

    def copies(step, slot):
        columns = pl.ds(pl.multiple_of(step * wide, 128), wide)
        return [
            pltpu.make_async_copy(piece.at[:, columns], w_ref.at[slot, where], sems.at[slot, i])
            for i, (piece, where) in enumerate(rows)
        ]

    @pl.when(step == 0)
    def _():
        for copy in [*loads, *copies(0, 0)]:
            copy.start()
        for load in loads:
            load.wait()

    for copy in copies(step, slot):
        copy.wait()

    @pl.when(step + 1 < steps)
    def _():
        for copy in copies(step + 1, 1 - slot):
            copy.start()

    weight = lambda at, width: w_ref[slot, :, at : at + width]
    attend_some(heads, place_ref[0] > 0, x_ref, lat_ref, rope_ref, weight, out_ref, peak_ref.at[0])


def attend(rows_of, groups, first, name, place, x, latents, rope, pieces, before=()):
    heads, steps, count, away = groups[0], len(groups), len(pieces), bool(before)
    own = (x, latents, rope)
    return pl.pallas_call(
        functools.partial(attend_kernel, rows_of, heads, steps, count, away),
        grid=(steps,),
        in_specs=[SMEM] + [ANY if away else VMEM] * 3 + [ANY] * (count + len(before)),
        out_specs=[
            pl.BlockSpec((TOK, heads * V_DIM), lambda p: (0, first // heads + p)),
            pl.BlockSpec((1, 8, 128), lambda p: (p, 0, 0)),
        ],
        out_shape=[
            jax.ShapeDtypeStruct((TOK, (HEADS_A + HEADS_B) * V_DIM), jnp.bfloat16),
            jax.ShapeDtypeStruct((steps, 8, 128), jnp.float32),
        ],
        input_output_aliases={4 + count: 0} if before else {},
        scratch_shapes=[
            pltpu.VMEM((2, TOK, heads * WIDE), jnp.bfloat16),
            pltpu.SemaphoreType.DMA((2, count)),
            pltpu.SemaphoreType.DMA((3,)),
        ]
        + [pltpu.VMEM(a.shape, a.dtype) for a in (own if away else ())],
        compiler_params=pltpu.CompilerParams(vmem_limit_bytes=20 * MIB),
        cost_estimate=pl.CostEstimate(
            flops=900_000_000 * heads * steps,
            bytes_accessed=1_000_000 * heads * steps,
            transcendentals=500_000 * heads * steps,
        ),
        name=name,
    )(place, *[in_hbm(a) if away else a for a in own], *pieces, *before)


def pack_kernel(q_ref, k_ref, v_ref, a_ref, b_ref):
    head = 0
    for groups, ref in ((GROUPS_A, a_ref), (GROUPS_B, b_ref)):
        at = 0
        for heads in groups:
            for j in range(3):
                columns = slice(head * HEAD, (head + heads) * HEAD)
                ref[:, at : at + heads * HEAD] = q_ref[8 * j : 8 * j + 8, columns]
                at += heads * HEAD
            for source in (k_ref, v_ref):
                ref[:, at : at + heads * QK_NOPE] = source[:, head * QK_NOPE : (head + heads) * QK_NOPE]
                at += heads * QK_NOPE
            head += heads


def pack(*weights):
    shapes = [jax.ShapeDtypeStruct((8, heads * WIDE), jnp.bfloat16) for heads in (HEADS_A, HEADS_B)]
    return pl.pallas_call(
        pack_kernel,
        grid=(1,),
        in_specs=[whole(a.shape) for a in weights],
        out_specs=[whole(a.shape) for a in shapes],
        out_shape=shapes,
        compiler_params=pltpu.CompilerParams(vmem_limit_bytes=8 * MIB),
        name="pack",
    )(*[in_hbm(a) for a in weights])


def order_kernel(offsets, me_ref, *refs):
    pieces, out_ref = refs[:-1], refs[-1]
    count = len(pieces)
    for offset, piece in zip(offsets, pieces):
        out_ref[lax.rem(me_ref[0] + offset % count, count)] = piece[...]


def in_order(me, offsets, pieces):
    rows, columns = pieces[0].shape
    count = len(pieces)
    return pl.pallas_call(
        functools.partial(order_kernel, offsets),
        in_specs=[SMEM] + [VMEM] * count,
        out_specs=VMEM,
        out_shape=jax.ShapeDtypeStruct((count, rows, columns), jnp.bfloat16),
        compiler_params=pltpu.CompilerParams(vmem_limit_bytes=4 * MIB),
        name="in_order",
    )(me.reshape(1), *pieces).reshape(count * rows, columns)


def halves_kernel(before_ref, after_ref, low_ref, high_ref):
    low_ref[...] = before_ref[:32]
    high_ref[...] = after_ref[32:]


def halves(before, after):
    shape = jax.ShapeDtypeStruct((32, before.shape[1]), before.dtype)
    return pl.pallas_call(
        halves_kernel,
        in_specs=[VMEM] * 2,
        out_specs=[VMEM] * 2,
        out_shape=[shape, shape],
        compiler_params=pltpu.CompilerParams(vmem_limit_bytes=4 * MIB),
        name="halves",
    )(before, after)


def one_hot(source, first):
    at = lax.broadcasted_iota(jnp.int32, (128, source.shape[1]), 0) + first
    return jnp.where(at == source, 1.0, 0.0).astype(jnp.bfloat16)


def picked(rows, tiles, source):
    left = jnp.concatenate([rows(tile) for tile in tiles], axis=1)
    right = jnp.concatenate([one_hot(source, tile * 128) for tile in tiles], axis=0)
    return dot_f32(left, right).astype(jnp.bfloat16)


def late_source(c, tile, strip):
    z, core, xh, xl, r = 2 * tile + ((c >> 6) & 1), (c >> 5) & 1, (c >> 4) & 1, (c >> 3) & 1, c & 7
    return ((xh * 2 + core) * 16 + z * 2 + xl) * strip + r


def early_source(c, tile, strip):
    core, z, r = (c >> 6) & 1, (c >> 3) & 7, c & 7
    return ((tile // 2 * 2 + core) * 16 + z * 2 + tile % 2) * strip + r


def order_query_kernel(x_ref, late_ref, early_ref):
    column = lax.broadcasted_iota(jnp.int32, (1, 384), 1)
    c, j = column & 127, column >> 7
    rows = lambda tile: x_ref[:, tile * 128 : (tile + 1) * 128]
    for tile in range(4):
        low, high = 96 * tile // 128, (96 * tile + 95) // 128
        near = [3 * block + part for block in range(4) for part in range(low, high + 1)]
        late = picked(rows, near, late_source(c, tile, 24) + 8 * j)
        near = [3 * (tile // 2 * 2 + core) + part for core in range(2) for part in range(3)]
        early = picked(rows, near, early_source(c, tile, 24) + 8 * j)
        for strip in range(3):
            late_ref[strip, :, tile * 128 : (tile + 1) * 128] = late[:, strip * 128 : (strip + 1) * 128]
            early_ref[strip, :, tile * 128 : (tile + 1) * 128] = early[:, strip * 128 : (strip + 1) * 128]


def order_query(x):
    shape = jax.ShapeDtypeStruct((3, TOK, 512), jnp.bfloat16)
    return pl.pallas_call(
        order_query_kernel,
        grid=(1,),
        in_specs=[whole(x.shape)],
        out_specs=[whole(shape.shape)] * 2,
        out_shape=[shape, shape],
        compiler_params=pltpu.CompilerParams(vmem_limit_bytes=16 * MIB),
        cost_estimate=pl.CostEstimate(flops=2_500_000_000, bytes_accessed=6_000_000, transcendentals=0),
        name="order_query",
    )(x)


def order_latent_kernel(me_ref, own_ref, own_rope_ref, *refs):
    pieces, (late_ref, early_ref, rope_ref, prev_ref) = refs[:4], refs[4:]
    for offset, piece in zip((0, -1, 1, 2), pieces):
        slot = lax.rem(me_ref[0] + offset % 4, 4)
        prev_ref[pl.ds(pl.multiple_of(slot * 128, 128), 128), :] = piece[...]
    rope_ref[:TOK] = own_rope_ref[...]
    rope_ref[TOK:] = prev_ref[:, 512:]
    c = lax.broadcasted_iota(jnp.int32, (1, 128), 1)
    for part, ref in ((0, own_ref), (1, prev_ref)):
        rows = lambda tile: ref[:, tile * 128 : (tile + 1) * 128]
        for tile in range(4):
            at = slice(tile * 128, (tile + 1) * 128)
            late_ref[part * TOK : (part + 1) * TOK, at] = picked(rows, range(4), late_source(c, tile, 8))
            near = [tile // 2 * 2, tile // 2 * 2 + 1]
            early_ref[part * TOK : (part + 1) * TOK, at] = picked(rows, near, early_source(c, tile, 8))


def order_latent(me, own, own_rope, pieces):
    operands = (own, own_rope, *pieces)
    shapes = [jax.ShapeDtypeStruct((2 * TOK, width), jnp.bfloat16) for width in (512, 512, QK_ROPE)]
    return pl.pallas_call(
        order_latent_kernel,
        grid=(1,),
        in_specs=[SMEM] + [whole(a.shape) for a in operands],
        out_specs=[whole(a.shape) for a in shapes],
        out_shape=shapes,
        scratch_shapes=[pltpu.VMEM((TOK, 512 + QK_ROPE), jnp.bfloat16)],
        compiler_params=pltpu.CompilerParams(vmem_limit_bytes=16 * MIB),
        cost_estimate=pl.CostEstimate(flops=1_000_000_000, bytes_accessed=4_000_000, transcendentals=0),
        name="order_latent",
    )(me.reshape(1), *operands)


def moved(block, axes, distance):
    count = lax.axis_size(axes)
    return lax.ppermute(block, axes, [(i, (i + distance) % count) for i in range(count)])


def local(query_latent, shared_latent, rope_keys, block_order, query_weight, key_weight, value_weight):
    heads = key_weight.shape[1] // QK_NOPE
    me_x = lax.axis_index(X).astype(jnp.int32)
    me_z = lax.axis_index("z").astype(jnp.int32)
    me_core = lax.axis_index("core").astype(jnp.int32)
    cycle = lax.axis_size(("z", "xl"))
    packed_a, packed_b = pack(query_weight, key_weight, value_weight)

    barrier = lax.optimization_barrier
    me_t = lax.axis_index("tensor").astype(jnp.int32)
    quarter = TOK // lax.axis_size("tensor")

    along_x = [packed_a, moved(packed_a, X, 1), moved(packed_a, X, -1), moved(packed_a, X, 2)]
    shard_a = in_order(me_x, (0, -1, 1, 2), along_x)
    shard_a, latent, rope_own, block_order = barrier((shard_a, shared_latent[0], rope_keys[0], block_order))
    gathered_a = lax.all_gather(shard_a, ("z", "core"), axis=0, tiled=True)

    position = lax.axis_index(("z", "xl"))
    order_row = block_order[lax.axis_index(("xh", "core"))]
    seen = (order_row[(position - 1 + cycle) % cycle] < order_row[position]).astype(jnp.int32)
    place = jnp.stack([seen, me_x, me_core])
    mine = jnp.concatenate(
        [lax.dynamic_slice_in_dim(a, me_t * quarter, quarter, 0) for a in (latent, rope_own)], axis=1
    )
    up, down = moved(packed_b, "z", 1), moved(packed_b, "z", -1)
    up2, down2 = moved(packed_b, "z", 2), moved(packed_b, "z", -2)
    up3, down3 = moved(up2, "z", 1), moved(down2, "z", -1)
    down4 = moved(down3, "z", -1)
    own = in_order(me_z, (0, -1, 1, -2, 2, -3, 3, 4), [packed_b, up, down, up2, down2, up3, down3, down4])
    theirs = moved(mine, ("z", "xl"), 1)
    own, theirs, place, rope_own = barrier((own, theirs, place, rope_own))

    before, after = moved(own, X, 1), moved(own, X, -1)
    prev = [theirs, moved(theirs, "tensor", 1), moved(theirs, "tensor", -1), moved(theirs, "tensor", 2)]
    x_a, x_b = order_query(query_latent[0])
    before, after, x_a, x_b = barrier((before, after, x_a, x_b))
    low, high = halves(before, after)
    far_low, far_high = moved(low, X, 1), moved(high, X, -1)
    lat_a, lat_b, rope = order_latent(me_t, latent, rope_own, prev)
    far_low, far_high, lat_a, lat_b, rope = barrier((far_low, far_high, lat_a, lat_b, rope))
    mine = [own, before, after, far_low, far_high]
    pieces = mine + [moved(piece, "core", 1) for piece in mine]

    out, peaks_b = attend(from_ring, GROUPS_B, HEADS_A, "ringed", place, x_b, lat_b, rope, pieces)
    gathered_a = [in_hbm(gathered_a)]
    attended, peaks_a = attend(from_gathered, GROUPS_A, 0, "gathered", place, x_a, lat_a, rope, gathered_a, [out])

    peaks = jnp.concatenate([peaks_a, peaks_b])[:, : GROUPS_A[0], 0].reshape(1, heads)
    everyone = lax.axis_size(GROUP)
    shared = lax.all_to_all(jnp.broadcast_to(peaks[None], (everyone, 1, heads)), GROUP, 0, 0)
    logit_max = jnp.max(shared, axis=(0, 1))
    clip = TAU / jnp.maximum(logit_max, TAU)
    root = jnp.sqrt(clip)
    factors = jnp.concatenate(
        [jnp.broadcast_to(root[:, None], (heads, QK_NOPE)), jnp.broadcast_to(clip[:, None], (heads, QK_ROPE))], axis=1
    ).reshape(1, heads * HEAD)
    clipped_q = (query_weight.astype(jnp.float32) * factors).astype(jnp.bfloat16)
    clipped_k = (key_weight.astype(jnp.float32) * jnp.repeat(root, QK_NOPE)[None]).astype(jnp.bfloat16)
    return (attended[None], logit_max, clipped_q, clipped_k)


def solution(mesh):
    fine = Mesh(mesh.devices.reshape(2, 2, 8, 2, 4), ("xh", "core", "z", "xl", "tensor"))
    dp, ctx = ("xh", "core"), ("z", "xl")
    return jax.shard_map(
        local,
        mesh=fine,
        in_specs=(
            P(dp, ctx, None),
            P(dp, ctx, None),
            P(dp, ctx, None),
            P(),
            P(GROUP, "tensor"),
            P(GROUP, "tensor"),
            P(GROUP, "tensor"),
        ),
        out_specs=(
            P(dp, ctx, "tensor"),
            P("tensor"),
            P(GROUP, "tensor"),
            P(GROUP, "tensor"),
        ),
        check_vma=False,
    )
```
